512 devices in a mesh: dp: 8 (over y, x_hi), expert: 64 (over x_lo, z, core).
Axes of the slice: x: 4 (x_hi: 2, x_lo: 2; x = x_hi * 2 + x_lo), y: 4, z: 16, core: 2. Of those that a mesh axis runs over, the one named last changes fastest.
Arguments:
- tokens: bfloat16 [8192, 3584], P('expert'), may hold values from -6 to 6
- routes: int32 [8192, 2], P('expert'), may hold values from 0 to 31, all different within a row; in each aligned block of 128 rows (0 to 127, 128 to 255, ...) at most 10 rows name the same one
- gate_weights: float32 [8192, 2], P('expert'), may hold values from 0.2 to 1
- w_dense_gate: bfloat16 [3584, 2432], P('expert', 'dp'), may hold values from -0.09375 to 0.09375
- w_dense_up: bfloat16 [3584, 2432], P('expert', 'dp'), may hold values from -0.09375 to 0.09375
- w_dense_down: bfloat16 [2432, 3584], P('dp', 'expert'), may hold values from -0.125 to 0.125
- w_exp_gate: bfloat16 [8, 64, 3584, 152], P('dp', 'expert'), may hold values from -0.09375 to 0.09375
- w_exp_up: bfloat16 [8, 64, 3584, 152], P('dp', 'expert'), may hold values from -0.09375 to 0.09375
- w_exp_down: bfloat16 [8, 64, 152, 3584], P('dp', 'expert'), may hold values from -0.125 to 0.125
Outputs:
- mixed: bfloat16 [8192, 3584], P('expert', 'dp')
The draws below stay inside these ranges and needn't reach their ends.
Inputs may be any that keep to these rules, and one draw needn't show every extreme that they name: `routes`: the two experts of a token differ. Among the rows of one device, no expert is named more than 10 times, and in every draw some expert is named exactly 10 times by some device's rows.
All inputs are finite; a program needn't handle non-finite values.
Results may differ from the reference program's by a relative error of at most 0.019.
Values may be sent and summed in bfloat16 or wider, within the bound.
A program may use at most 128 MiB of HBM per device.

```python
import math
import jax
import jax.numpy as jnp
import numpy as np
from jax import lax

D = 3584
DFF = 2432
FF_E = 2432
TOK_DEV = 128
TOP = 2
EXPERTS = 32
CAP = 10
HID_DEV = 152
TOKENS = 8192
N_DP = 8
N_EXPERT = 64


def level_of(own_key, dims, cuts, low, top_value):
    def one(axis_at, parts):
        steps = jax.random.uniform(jax.random.fold_in(jax.random.fold_in(own_key, 6), axis_at), (parts,), jnp.float32, low / len(cuts), top_value / len(cuts))
        return jnp.repeat(jnp.exp(steps), dims[axis_at] // parts).reshape((-1,) + (1,) * (len(dims) - axis_at - 1))

    gain = one(*cuts[0])
    for cut in cuts[1:]:
        gain = gain * one(*cut)
    return gain


def assign_block(own_key, own, number, rows, number_of, top, bound, skew):
    order = jax.random.permutation(own_key, number_of)
    heavy_load, ordinary = shares(number_of, rows * top, bound, skew, True), shares(number_of, rows * top, bound, skew, False)
    places = jnp.arange(number_of)

    def named(tallies, rotation):
        used = int((tallies > 0).sum())
        fixed = max(1, used // 4)
        shifted = fixed + (places - fixed + rotation * (used - fixed)) % max(1, number_of - fixed)
        return jnp.zeros((number_of,), jnp.int32).at[order[jnp.where(places < fixed, places, shifted)]].set(jnp.asarray(tallies, jnp.int32))

    tallies = jnp.where(number % 4 == 0, named(heavy_load, number // 4), named(ordinary, number - number // 4 - 1))
    mixed = jax.random.permutation(jax.random.fold_in(own, 3), number_of)
    source_of, sink = mixed[0:number_of // 2 * 2:2], mixed[1:number_of // 2 * 2:2]
    margin = jnp.minimum(tallies[source_of] - 1, bound - tallies[sink]) // 2
    margin = jnp.where((source_of == order[0]) | (sink == order[0]) | (tallies[sink] == 0), 0, jnp.maximum(margin, 0))
    shifted = jax.random.randint(jax.random.fold_in(own, 4), (number_of // 2,), 0, 1 << 20) % (margin + 1)
    tallies = tallies.at[source_of].add(-shifted).at[sink].add(shifted)
    items = jnp.searchsorted(jnp.cumsum(tallies), jnp.arange(rows * top), side="right").astype(jnp.int32)
    listing = items.reshape(top, rows).T
    listing = listing[jax.random.permutation(jax.random.fold_in(own, 1), rows)]
    rotation = jax.random.randint(jax.random.fold_in(own, 2), (rows, 1), 0, top)
    return jnp.take_along_axis(listing, (jnp.arange(top)[None, :] + rotation) % top, axis=1)


def shares(number_of, total, most, slope, full):
    portions = [(1 << 20) // math.isqrt(grade ** slope) + 1 for grade in range(1, number_of + 1)]
    largest = most if full else min(most, max(-(-total // number_of), total * portions[0] // sum(portions)))
    least = 1 if total - largest >= number_of - 1 else 0
    holding, rest = [largest] + [least] * (number_of - 1), total - largest - least * (number_of - 1)
    while rest > 0:
        candidates = [i for i in range(1, number_of) if holding[i] < largest] or [i for i in range(1, number_of) if holding[i] < most]
        mass, budget = sum([portions[i] for i in candidates]), rest
        for i in candidates:
            extra = min(most - holding[i], max(1, budget * portions[i] // mass), rest)
            holding[i] = holding[i] + extra
            rest = rest - extra
    return np.array(holding)


def scatter_about(own_key, dims, scale, most, pieces=(), kind=jnp.bfloat16):
    drawn = jax.random.normal(own_key, dims, jnp.float32) * scale
    if len(pieces) > 0:
        drawn = level_of(own_key, dims, pieces, -0.22, 0.18) * drawn
    return jnp.clip(drawn, min=-most, max=most).astype(kind)


def setup_inputs(seed: int = 0) -> dict:
    keys = jax.random.split(jax.random.key(seed), 10)
    tokens = scatter_about(keys[0], (TOKENS, D), 1.0, 6.0, ((0, 64),))
    routes_keys = jax.random.split(jax.random.fold_in(keys[1], 1), TOKENS // TOK_DEV)
    routes_turns = jax.random.permutation(jax.random.fold_in(keys[1], 3), TOKENS // TOK_DEV)
    routes = jax.vmap(lambda own, number: assign_block(jax.random.fold_in(keys[1], 2), own, number, TOK_DEV, EXPERTS, TOP, CAP, 2))(routes_keys, routes_turns).reshape((TOKENS, TOP))
    gate_weights = jnp.clip(0.2 + 0.8 * jax.random.uniform(keys[2], (TOKENS, TOP), jnp.float32) ** level_of(keys[2], (TOKENS, TOP), ((0, 64),), -0.2, 0.2), 0.2, 1.0)
    w_dense_gate = scatter_about(keys[3], (D, DFF), D ** -0.5, 0.09375, ((0, 64), (1, 8)))
    w_dense_up = scatter_about(keys[4], (D, DFF), D ** -0.5, 0.09375, ((0, 64), (1, 8)))
    w_dense_down = scatter_about(keys[5], (DFF, D), DFF ** -0.5, 0.125, ((0, 8), (1, 64)))
    w_exp_gate = scatter_about(keys[6], (N_DP, N_EXPERT, D, HID_DEV), D ** -0.5, 0.09375, ((0, 8), (1, 64)))
    w_exp_up = scatter_about(keys[7], (N_DP, N_EXPERT, D, HID_DEV), D ** -0.5, 0.09375, ((0, 8), (1, 64)))
    w_exp_down = scatter_about(keys[8], (N_DP, N_EXPERT, HID_DEV, D), FF_E ** -0.5, 0.125, ((0, 8), (1, 64)))
    return dict(tokens=tokens, routes=routes, gate_weights=gate_weights, w_dense_gate=w_dense_gate, w_dense_up=w_dense_up, w_dense_down=w_dense_down, w_exp_gate=w_exp_gate, w_exp_up=w_exp_up, w_exp_down=w_exp_down)


def reference(tokens, routes, gate_weights, w_dense_gate, w_dense_up, w_dense_down, w_exp_gate, w_exp_up, w_exp_down):
    dense_gate = jnp.dot(tokens, w_dense_gate, preferred_element_type=jnp.float32)
    dense_up = jnp.dot(tokens, w_dense_up, preferred_element_type=jnp.float32)
    dense_hidden = (jax.nn.silu(dense_gate) * dense_up).astype(jnp.bfloat16)
    flat_route = routes.reshape(-1).astype(jnp.int32)
    total = TOKENS * TOP
    owner_token = (jnp.arange(total, dtype=jnp.int32) // TOP).astype(jnp.int32)
    limit = CAP * N_EXPERT
    slab = DFF // N_DP
    mixed_sum = jnp.zeros((TOKENS, D), jnp.float32)
    for block in range(N_DP):
        hid_block = dense_hidden[:, block * slab:(block + 1) * slab]
        down_block = w_dense_down[block * slab:(block + 1) * slab, :]
        dense_part = jnp.dot(hid_block, down_block, preferred_element_type=jnp.float32)
        gate_block = w_exp_gate[block]
        up_block = w_exp_up[block]
        exp_down_block = w_exp_down[block]

        def one_expert(carry, expert):
            found = jnp.nonzero(flat_route == expert, size=limit, fill_value=total)[0].astype(jnp.int32)
            rows = tokens[owner_token[jnp.minimum(found, total - 1)]]
            summed = jnp.zeros((limit, D), jnp.float32)
            for half in range(2):
                place = 2 * expert + half
                gate = jnp.dot(rows, gate_block[place], preferred_element_type=jnp.float32)
                up = jnp.dot(rows, up_block[place], preferred_element_type=jnp.float32)
                hidden = (jax.nn.silu(gate) * up).astype(jnp.bfloat16)
                summed = summed + jnp.dot(hidden, exp_down_block[place], preferred_element_type=jnp.float32)
            part = summed.astype(jnp.bfloat16).astype(jnp.float32)
            carry = carry.at[found].set(part, mode="drop")
            return carry, None

        routed = jnp.zeros((total, D), jnp.float32)
        routed, _ = lax.scan(one_expert, routed, jnp.arange(EXPERTS, dtype=jnp.int32))
        weighted = jnp.sum(gate_weights[:, :, None] * routed.reshape(TOKENS, TOP, D), axis=1)
        slice_term = (dense_part + weighted).astype(jnp.bfloat16)
        mixed_sum = mixed_sum + slice_term.astype(jnp.float32)
    return mixed_sum.astype(jnp.bfloat16)
```

```python
import jax
import jax.numpy as jnp
from jax import lax
from jax.sharding import Mesh, PartitionSpec as P

TOP = 2
CAP = 10


def per_device(
    tokens,
    routes,
    gate_weights,
    w_dense_gate,
    w_dense_up,
    w_dense_down,
    w_exp_gate,
    w_exp_up,
    w_exp_down,
):
    tok_rows, width = tokens.shape
    n_dp = lax.axis_size("dp")
    groups = lax.axis_size("group")
    devices = 2 * groups
    part = width // n_dp
    half = part // 2
    places = groups * CAP
    me_dp = lax.axis_index("dp")

    flat_route = routes.reshape(-1)
    owners = (flat_route[:, None] == jnp.arange(groups, dtype=jnp.int32)[None, :]).astype(jnp.int32)
    earlier = jnp.cumsum(owners, axis=0) - owners
    ranking = jnp.sum(earlier * owners, axis=1)
    target = flat_route * CAP + ranking
    selector = target[:, None] == jnp.arange(places, dtype=jnp.int32)[None, :]
    selector = selector.reshape(tok_rows, TOP, places)
    token_select = jnp.sum(selector.astype(jnp.bfloat16), axis=1)

    mine = lax.dynamic_slice_in_dim(tokens, me_dp * part, part, axis=1)
    outgoing = jnp.einsum("tp,td->pd", token_select, mine, preferred_element_type=jnp.float32)
    outgoing = outgoing.astype(jnp.bfloat16).reshape(groups, CAP, 2, half)
    outgoing = outgoing.transpose(0, 2, 1, 3).reshape(devices, CAP, half)
    arrived = lax.all_to_all(outgoing, ("group", "core"), split_axis=0, concat_axis=0, tiled=True)
    rows = arrived.reshape(devices * CAP, half)
    allcols = lax.all_gather(rows, ("dp", "core"), axis=0, tiled=False)
    allcols = allcols.reshape(n_dp * 2, devices * CAP, half)
    x = allcols.transpose(1, 0, 2).reshape(devices * CAP, width)
    gate = jnp.dot(x, w_exp_gate[0, 0], preferred_element_type=jnp.float32)
    up = jnp.dot(x, w_exp_up[0, 0], preferred_element_type=jnp.float32)
    hidden = (jax.nn.silu(gate) * up).astype(jnp.bfloat16)
    result = jnp.dot(hidden, w_exp_down[0, 0], preferred_element_type=jnp.float32)
    result = result.astype(jnp.bfloat16)
    summed = lax.psum_scatter(result, ("dp", "core"), scatter_dimension=1, tiled=True)
    summed = summed.reshape(devices, CAP, half)
    returned = lax.all_to_all(summed, ("group", "core"), split_axis=0, concat_axis=0, tiled=True)
    returned = returned.reshape(groups, 2, CAP, half).transpose(0, 2, 1, 3).reshape(places, part)
    mix = jnp.sum(selector.astype(jnp.float32) * gate_weights[:, :, None], axis=1)
    weighted = jnp.dot(mix, returned.astype(jnp.float32), preferred_element_type=jnp.float32)

    tok_axes = ("group", "core")
    dense_gate = jnp.dot(
        tokens,
        lax.all_gather(w_dense_gate, tok_axes, axis=0, tiled=True),
        preferred_element_type=jnp.float32,
    )
    dense_up = jnp.dot(
        tokens,
        lax.all_gather(w_dense_up, tok_axes, axis=0, tiled=True),
        preferred_element_type=jnp.float32,
    )
    dense_hidden = (jax.nn.silu(dense_gate) * dense_up).astype(jnp.bfloat16)
    dense_part = jnp.dot(
        dense_hidden,
        lax.all_gather(w_dense_down, tok_axes, axis=1, tiled=True),
        preferred_element_type=jnp.float32,
    )
    dense = lax.psum_scatter(
        dense_part.astype(jnp.bfloat16), "dp", scatter_dimension=1, tiled=True
    )
    return (dense.astype(jnp.float32) + weighted).astype(jnp.bfloat16)


def solution(mesh):
    n_dp, n_expert = mesh.devices.shape
    fine = Mesh(mesh.devices.reshape(n_dp, n_expert // 2, 2), ("dp", "group", "core"))
    ex = ("group", "core")
    in_specs = (
        P(ex, None),
        P(ex, None),
        P(ex, None),
        P(ex, "dp"),
        P(ex, "dp"),
        P("dp", ex),
        P("dp", ex, None, None),
        P("dp", ex, None, None),
        P("dp", ex, None, None),
    )
    return jax.shard_map(
        per_device, mesh=fine, in_specs=in_specs, out_specs=P(ex, "dp"), check_vma=False
    )
```

```python
import functools

import jax
import jax.numpy as jnp
from jax import lax
from jax.experimental import pallas as pl
from jax.experimental.pallas import tpu as pltpu
from jax.sharding import PartitionSpec as P

CAP = 10
SLOT = 16
NZ = 16
NY = 4
NDP = 8
NT = 128
D = 3584
HH = 152
BLOCK = 8 * CAP
CHIP_ROWS = 112
COLS = 448
CHUNK = 512
MESH = pl.DeviceIdType.MESH
F32 = jnp.float32
BF16 = jnp.bfloat16


def dz_of(j, xl_to, i):
    d = jnp.where(xl_to == 0, j, 8 - j)
    edge = (d % 8) == 0
    first = jnp.where(edge, 0, d)
    second = jnp.where(edge, 8, NZ - d)
    return jnp.where(i == 0, first, second)


def kernel(
    routes, routes_t, weights, tok_hbm, pack_hbm, wg_hbm, wu_hbm, wd_hbm, out,
    tok2, sbuf, rbuf, xbuf, obuf, rsum, tbuf, ret, wg, wu, wd, mine, theirs, dense_w,
    d_mine, d_send, d_recv, term, fin,
    loc, core_send, core_recv, dis_send, dis_recv, bc_send, bc_recv,
    right_send, right_recv, left_send, left_recv, x_send, x_recv,
    rs_send, rs_recv, ret_send, ret_recv, fin_send, fin_recv,
):
    b = lax.axis_index("dp")
    ex = lax.axis_index("expert")
    core = ex % 2
    chip = ex // 2
    z = chip % NZ
    xl = chip // NZ
    y = b // 2
    active = (b % 2) == core
    j_me = (b + 15 - core) % 8

    def dev(bb, xx, zz, cc):
        return (bb, (xx * NZ + zz) * 2 + cc)

    def remote(src, dst, send, recv, to):
        return pltpu.make_async_remote_copy(
            src_ref=src, dst_ref=dst, send_sem=send, recv_sem=recv, device_id=to,
            device_id_type=MESH,
        )

    def dest_of(k):
        to_x, i = k // 2, k % 2
        return to_x, (z + dz_of(j_me, to_x, i)) % NZ

    def source_of(slot):
        i, s_x, s_c = slot // 4, (slot // 2) % 2, slot % 2
        j = (b + 15 - s_c) % 8
        return s_x, (z + NZ - dz_of(j, xl, i)) % NZ, s_c

    local = [
        pltpu.make_async_copy(tok_hbm, tok2.at[pl.ds(0, NT)], loc.at[0]),
        pltpu.make_async_copy(pack_hbm.at[core], mine, loc.at[1]),
        pltpu.make_async_copy(wg_hbm, wg.at[0], loc.at[2]),
        pltpu.make_async_copy(wu_hbm, wu.at[0], loc.at[3]),
        pltpu.make_async_copy(wd_hbm, wd.at[0], loc.at[4]),
    ]
    for copy in local:
        copy.start()

    barrier = pltpu.get_barrier_semaphore()

    def greet(to):
        pl.semaphore_signal(barrier, inc=1, device_id=to, device_id_type=MESH)

    @pl.loop(1, NDP)
    def _(k):
        greet(((b + k) % NDP, ex))

    partner = (b, chip * 2 + 1 - core)
    across = dev(b, 1 - xl, z, core)
    up_z = dev(b, xl, (z + 1) % NZ, core)
    down_z = dev(b, xl, (z + NZ - 1) % NZ, core)
    for to in (partner, across, up_z, down_z):
        greet(to)

    @pl.loop(0, 4)
    def _(k):
        to_x, to_z = dest_of(k)
        greet(dev(b, to_x, to_z, b % 2))

    @pl.when(active)
    def _():
        @pl.loop(0, 8)
        def _(s):
            s_x, s_z, s_c = source_of(s)
            greet(dev(b, s_x, s_z, s_c))

    pl.semaphore_wait(barrier, jnp.where(active, 7 + 4 + 4 + 8, 7 + 4 + 4))

    to_partner = [
        remote(pack_hbm.at[1 - core], theirs, core_send.at[0], core_recv.at[0], partner),
        remote(wg_hbm, wg.at[1], core_send.at[1], core_recv.at[1], partner),
        remote(wu_hbm, wu.at[1], core_send.at[2], core_recv.at[2], partner),
        remote(wd_hbm, wd.at[1], core_send.at[3], core_recv.at[3], partner),
        remote(tok_hbm, tok2.at[pl.ds(NT, NT)], core_send.at[4], core_recv.at[4], partner),
    ]
    for copy in to_partner:
        copy.start()

    row = lax.broadcasted_iota(jnp.int32, (4 * SLOT, NT), 0)
    k_row = row // SLOT
    e_row = (k_row // 2) * NZ + (z + dz_of(j_me, k_row // 2, k_row % 2)) % NZ
    hit = (routes_t[0:1, :] == e_row) | (routes_t[1:2, :] == e_row)
    before = (
        lax.broadcasted_iota(jnp.int32, (NT, NT), 0)
        < lax.broadcasted_iota(jnp.int32, (NT, NT), 1)
    )
    rank = jnp.dot(
        jnp.where(hit, 1.0, 0.0).astype(BF16),
        jnp.where(before, 1.0, 0.0).astype(BF16),
        preferred_element_type=F32,
    )
    select = jnp.where(hit & (rank == (row % SLOT).astype(F32)), 1.0, 0.0).astype(BF16)
    local[0].wait()
    for n in range(D // CHUNK):
        cols = pl.ds(n * CHUNK, CHUNK)
        sbuf[:, cols] = jnp.dot(
            select, tok2[0:NT, cols], preferred_element_type=F32
        ).astype(BF16)

    def dispatch(k):
        to_x, to_z = dest_of(k)
        slot = (k % 2) * 4 + xl * 2 + core
        return remote(
            sbuf.at[pl.ds(pl.multiple_of(k * SLOT, SLOT), SLOT)],
            rbuf.at[pl.ds(pl.multiple_of(slot * SLOT, SLOT), SLOT)],
            dis_send.at[k], dis_recv.at[slot], dev(b, to_x, to_z, b % 2),
        )

    @pl.loop(0, 4)
    def _(k):
        dispatch(k).start()

    local[1].wait()
    to_partner[0].wait_recv()

    def shard(xx, zz):
        start = (xx * NZ + zz) * CHIP_ROWS
        return dense_w.at[pl.ds(pl.multiple_of(start, 16), CHIP_ROWS)]

    first = jnp.where(core == 0, mine[...], theirs[...])
    second = jnp.where(core == 0, theirs[...], mine[...])
    dense_w[pl.ds(pl.multiple_of(chip * CHIP_ROWS, 16), CHIP_ROWS), :] = jnp.concatenate(
        [first, second], axis=0
    )

    slot_row = lax.broadcasted_iota(jnp.int32, (BLOCK, 8 * SLOT), 0)
    slot_col = lax.broadcasted_iota(jnp.int32, (BLOCK, 8 * SLOT), 1)
    squeeze = jnp.where(
        slot_col == (slot_row // CAP) * SLOT + slot_row % CAP, 1.0, 0.0
    ).astype(BF16)

    def spread(k):
        return remote(
            xbuf.at[y], xbuf.at[y], bc_send.at[k - 1], bc_recv.at[y], ((b + k) % NDP, ex)
        )

    @pl.when(active)
    def _():
        @pl.loop(0, 8)
        def _(s):
            remote(
                sbuf.at[pl.ds(0, SLOT)],
                rbuf.at[pl.ds(pl.multiple_of(s * SLOT, SLOT), SLOT)],
                dis_send.at[0], dis_recv.at[s], partner,
            ).wait_recv()

        for n in range(D // CHUNK):
            cols = pl.ds(n * CHUNK, CHUNK)
            xbuf[y, :, cols] = jnp.dot(
                squeeze, rbuf[:, cols], preferred_element_type=F32
            ).astype(BF16)

        @pl.loop(1, NDP)
        def _(k):
            spread(k).start()

    def go_right(k):
        s = shard(xl, (z + NZ - k) % NZ)
        return remote(s, s, right_send.at[k], right_recv.at[k], up_z)

    def go_left(k):
        s = shard(xl, (z + k) % NZ)
        return remote(s, s, left_send.at[k], left_recv.at[k], down_z)

    def go_across(k):
        s = shard(xl, (z + k) % NZ)
        return remote(s, s, x_send.at[k], x_recv.at[k], across)

    go_right(0).start()
    go_left(0).start()
    go_across(0).start()

    @pl.loop(1, 8)
    def _(k):
        go_right(k - 1).wait_recv()
        go_right(k).start()
        go_left(k - 1).wait_recv()

        @pl.when(k < 7)
        def _():
            go_left(k).start()

        go_across(NZ - k).start()
        go_across(k).start()

    go_right(7).wait_recv()
    go_across(8).start()

    for copy in local[2:]:
        copy.wait()
    for copy in to_partner[1:4]:
        copy.wait_recv()

    def back(yy):
        return remote(
            obuf.at[yy], rsum.at[b], rs_send.at[yy], rs_recv.at[b], (2 * yy + core, ex)
        )

    @pl.loop(0, NY)
    def _(k):
        yy = (y + k) % NY
        foreign = jnp.logical_not(active & (k == 0))

        @pl.when(foreign)
        def _():
            remote(
                xbuf.at[yy], xbuf.at[yy], bc_send.at[0], bc_recv.at[yy], partner
            ).wait_recv()

        x = xbuf[yy]
        hidden = []
        for h in range(2):
            gate = jnp.dot(x, wg[h], preferred_element_type=F32)
            up = jnp.dot(x, wu[h], preferred_element_type=F32)
            hidden.append((gate / (1.0 + jnp.exp(-gate)) * up).astype(BF16))
        for n in range(D // CHUNK):
            cols = pl.ds(n * CHUNK, CHUNK)
            obuf[yy, :, cols] = (
                jnp.dot(hidden[0], wd[0, :, cols], preferred_element_type=F32)
                + jnp.dot(hidden[1], wd[1, :, cols], preferred_element_type=F32)
            ).astype(BF16)

        @pl.when(foreign)
        def _():
            back(yy).start()

    to_partner[4].wait_recv()

    @pl.loop(0, NZ)
    def _(k):
        s = shard(1 - xl, (z + k) % NZ)
        remote(s, s, x_send.at[k], x_recv.at[k], across).wait_recv()

    both = jnp.dot(tok2[...], dense_w[:, 0:384], preferred_element_type=F32)
    ups = pltpu.roll(both, 384 - HH, 1)
    dense_hidden = both / (1.0 + jnp.exp(-both)) * ups
    lane = lax.broadcasted_iota(jnp.int32, (2 * NT, 384), 1)
    dense_hidden = jnp.where(lane < HH, dense_hidden, 0.0)
    placed = pltpu.roll(dense_hidden, 2 * HH - 256, 1)[:, 0:256].astype(BF16)
    for n in range(D // CHUNK):
        part = lax.dot_general(
            placed,
            dense_w[n * CHUNK:(n + 1) * CHUNK, 256:512],
            (((1,), (1,)), ((), ())),
            preferred_element_type=F32,
        )
        cols = pl.ds(n * CHUNK, CHUNK)
        d_mine[:, cols] = part[0:NT]
        d_send[:, cols] = part[NT:2 * NT].astype(BF16)
    swap = remote(d_send, d_recv, core_send.at[5], core_recv.at[5], partner)
    swap.start()

    def give(s):
        s_x, s_z, s_c = source_of(s)
        k = xl * 2 + s // 4
        return remote(
            tbuf.at[pl.ds(pl.multiple_of(s * SLOT, SLOT), SLOT)],
            ret.at[pl.ds(pl.multiple_of(k * SLOT, SLOT), SLOT)],
            ret_send.at[s], ret_recv.at[k], dev(b, s_x, s_z, s_c),
        )

    @pl.when(active)
    def _():
        @pl.loop(1, NDP)
        def _(k):
            src = (b + k) % NDP
            remote(
                obuf.at[0], rsum.at[src], rs_send.at[0], rs_recv.at[src], partner
            ).wait_recv()

        widen = jnp.where(
            lax.broadcasted_iota(jnp.int32, (8 * SLOT, BLOCK), 0)
            == (lax.broadcasted_iota(jnp.int32, (8 * SLOT, BLOCK), 1) // CAP) * SLOT
            + lax.broadcasted_iota(jnp.int32, (8 * SLOT, BLOCK), 1) % CAP,
            1.0, 0.0,
        ).astype(BF16)
        for n in range(D // CHUNK):
            cols = pl.ds(n * CHUNK, CHUNK)
            total = obuf[y, :, cols].astype(F32)
            for k in range(1, NDP):
                total = total + rsum[(b + k) % NDP, :, cols].astype(F32)
            tbuf[:, cols] = jnp.dot(
                widen, total.astype(BF16), preferred_element_type=F32
            ).astype(BF16)

        @pl.loop(0, 8)
        def _(s):
            give(s).start()

    col = lax.broadcasted_iota(jnp.int32, (NT, 4 * SLOT), 1)
    k_col = col // SLOT
    e_col = (k_col // 2) * NZ + (z + dz_of(j_me, k_col // 2, k_col % 2)) % NZ
    hit0 = routes[:, 0:1] == e_col
    hit1 = routes[:, 1:2] == e_col
    earlier = (
        lax.broadcasted_iota(jnp.int32, (NT, NT), 1)
        < lax.broadcasted_iota(jnp.int32, (NT, NT), 0)
    )
    rank_col = jnp.dot(
        jnp.where(earlier, 1.0, 0.0).astype(BF16),
        jnp.where(hit0 | hit1, 1.0, 0.0).astype(BF16),
        preferred_element_type=F32,
    )
    share = jnp.where(hit0, weights[:, 0:1], 0.0) + jnp.where(hit1, weights[:, 1:2], 0.0)
    share = jnp.where(rank_col == (col % SLOT).astype(F32), share, 0.0)
    share_hi = share.astype(BF16)
    share_lo = (share - share_hi.astype(F32)).astype(BF16)

    swap.wait_recv()

    @pl.loop(0, 4)
    def _(k):
        remote(
            tbuf.at[pl.ds(0, SLOT)],
            ret.at[pl.ds(pl.multiple_of(k * SLOT, SLOT), SLOT)],
            ret_send.at[0], ret_recv.at[k], partner,
        ).wait_recv()

    for n in range(NDP // 2):
        cols = pl.ds(n * 2 * COLS, 2 * COLS)
        rows = ret[:, cols]
        value = (
            d_mine[:, cols]
            + d_recv[:, cols].astype(F32)
            + jnp.dot(share_hi, rows, preferred_element_type=F32)
            + jnp.dot(share_lo, rows, preferred_element_type=F32)
        ).astype(BF16)
        term[2 * n] = value[:, 0:COLS]
        term[2 * n + 1] = value[:, COLS:2 * COLS]

    def finish(k):
        to = (b + k) % NDP
        return remote(
            term.at[to], fin.at[b], fin_send.at[k - 1], fin_recv.at[b], (to, ex)
        )

    @pl.loop(1, NDP)
    def _(k):
        finish(k).start()

    @pl.loop(1, NDP)
    def _(k):
        src = (b + k) % NDP
        remote(
            term.at[0], fin.at[src], fin_send.at[0], fin_recv.at[src], partner
        ).wait_recv()

    total = term[b].astype(F32)
    for k in range(1, NDP):
        total = total + fin[(b + k) % NDP].astype(F32)
    out[...] = total.astype(BF16)

    for copy in to_partner:
        copy.wait_send()
    swap.wait_send()

    @pl.loop(0, 4)
    def _(k):
        dispatch(k).wait_send()

    @pl.loop(0, 8)
    def _(k):
        go_right(k).wait_send()

    @pl.loop(0, 7)
    def _(k):
        go_left(k).wait_send()

    @pl.loop(0, NZ)
    def _(k):
        go_across(k).wait_send()

    @pl.loop(0, NY)
    def _(k):
        @pl.when(jnp.logical_not(active & (k == 0)))
        def _():
            back((y + k) % NY).wait_send()

    @pl.when(active)
    def _():
        @pl.loop(1, NDP)
        def _(k):
            spread(k).wait_send()

        @pl.loop(0, 8)
        def _(s):
            give(s).wait_send()

    @pl.loop(1, NDP)
    def _(k):
        finish(k).wait_send()


def per_device(
    tokens, routes, gate_weights, w_dense_gate, w_dense_up, w_dense_down,
    w_exp_gate, w_exp_up, w_exp_down,
):
    down_t = w_dense_down.T
    pad = jnp.zeros((w_dense_gate.shape[0], CHUNK - 3 * HH), BF16)
    pack = jnp.stack(
        [
            jnp.concatenate(
                [w[:, h * HH:(h + 1) * HH] for w in (w_dense_gate, w_dense_up, down_t)] + [pad],
                axis=1,
            )
            for h in range(2)
        ]
    )
    rows = w_dense_gate.shape[0]
    vmem = pl.BlockSpec(memory_space=pltpu.VMEM)
    hbm = pl.BlockSpec(memory_space=pl.ANY)
    dma = pltpu.SemaphoreType.DMA
    return pl.pallas_call(
        kernel,
        out_shape=jax.ShapeDtypeStruct((NT, COLS), BF16),
        in_specs=[vmem, vmem, vmem, hbm, hbm, hbm, hbm, hbm],
        out_specs=vmem,
        scratch_shapes=[
            pltpu.VMEM((2 * NT, D), BF16),
            pltpu.VMEM((4 * SLOT, D), BF16),
            pltpu.VMEM((8 * SLOT, D), BF16),
            pltpu.VMEM((NY, BLOCK, D), BF16),
            pltpu.VMEM((NY, BLOCK, D), BF16),
            pltpu.VMEM((NDP, BLOCK, D), BF16),
            pltpu.VMEM((8 * SLOT, D), BF16),
            pltpu.VMEM((4 * SLOT, D), BF16),
            pltpu.VMEM((2, D, HH), BF16),
            pltpu.VMEM((2, D, HH), BF16),
            pltpu.VMEM((2, HH, D), BF16),
            pltpu.VMEM((rows, CHUNK), BF16),
            pltpu.VMEM((rows, CHUNK), BF16),
            pltpu.VMEM((D, CHUNK), BF16),
            pltpu.VMEM((NT, D), F32),
            pltpu.VMEM((NT, D), BF16),
            pltpu.VMEM((NT, D), BF16),
            pltpu.VMEM((NDP, NT, COLS), BF16),
            pltpu.VMEM((NDP, NT, COLS), BF16),
            dma((5,)), dma((6,)), dma((6,)), dma((4,)), dma((8,)), dma((7,)), dma((4,)),
            dma((8,)), dma((8,)), dma((7,)), dma((7,)), dma((16,)), dma((16,)),
            dma((4,)), dma((8,)), dma((8,)), dma((4,)), dma((7,)), dma((8,)),
        ],
        compiler_params=pltpu.CompilerParams(
            collective_id=0, has_side_effects=True, vmem_limit_bytes=56 * 1024 * 1024
        ),
    )(
        routes, routes.T, gate_weights, tokens, pack,
        w_exp_gate[0, 0], w_exp_up[0, 0], w_exp_down[0, 0],
    )


def solution(mesh):
    in_specs = (
        P("expert", None),
        P("expert", None),
        P("expert", None),
        P("expert", "dp"),
        P("expert", "dp"),
        P("dp", "expert"),
        P("dp", "expert", None, None),
        P("dp", "expert", None, None),
        P("dp", "expert", None, None),
    )
    return jax.shard_map(
        per_device, mesh=mesh, in_specs=in_specs, out_specs=P("expert", "dp"), check_vma=False
    )
```

```python
import jax
import jax.numpy as jnp
from jax import lax
from jax.experimental import pallas as pl
from jax.experimental.pallas import tpu as pltpu
from jax.sharding import PartitionSpec as P

CAP = 10
SLOT = 16
NZ = 16
NY = 4
NDP = 8
NT = 128
D = 3584
HALF = D // 2
HH = 152
BLOCK = 8 * CAP
CHIP_ROWS = 112
COLS = 448
CHUNK = 512
PIECE = 256
EXPERTS = 32
MESH = pl.DeviceIdType.MESH
F32 = jnp.float32
BF16 = jnp.bfloat16


def dz_of(j, xl_to, i):
    d = jnp.where(xl_to == 0, j, 8 - j)
    edge = (d % 8) == 0
    first = jnp.where(edge, 0, d)
    second = jnp.where(edge, 8, NZ - d)
    return jnp.where(i == 0, first, second)


def iota(shape, dim):
    return lax.broadcasted_iota(jnp.int32, shape, dim)


def ones_where(mask):
    return jnp.where(mask, 1.0, 0.0).astype(BF16)


def dot(a, b):
    return jnp.dot(a, b, preferred_element_type=F32)


def dot_nt(a, b):
    return lax.dot_general(a, b, (((1,), (1,)), ((), ())), preferred_element_type=F32)


def silu(v):
    return v / (1.0 + jnp.exp(-v))


def kernel(
    routes_t, weights_t, dg, du, dd_t, tok_hbm, wg_hbm, wu_hbm, wd_hbm, out,
    tok, tq, sbuf, rbuf, xbuf, obuf, rsum, tbuf, ret, wg, wu, wd, pack, theirs, dense_w,
    gu, gu_send, gu_recv, hbuf, d_mine, d_send, d_recv, dterm, fin,
    loc, core_send, core_recv, ac_send, ac_recv, dis_send, dis_recv, bc_send, bc_recv,
    right_send, right_recv, left_send, left_recv,
    rs_send, rs_recv, ret_send, ret_recv, fin_send, fin_recv,
):
    b = lax.axis_index("dp")
    ex = lax.axis_index("expert")
    core = ex % 2
    chip = ex // 2
    z = chip % NZ
    xl = chip // NZ
    y = b // 2
    active = (b % 2) == core
    own_half = (b // 4) == xl

    def dev(bb, xx, zz, cc):
        return (bb, (xx * NZ + zz) * 2 + cc)

    def remote(src, dst, send, recv, to):
        return pltpu.make_async_remote_copy(
            src_ref=src, dst_ref=dst, send_sem=send, recv_sem=recv, device_id=to,
            device_id_type=MESH,
        )

    def dest_of(bb, k):
        to_x, i = k // 2, k % 2
        return to_x, (z + dz_of((bb + 15 - core) % 8, to_x, i)) % NZ

    def source_of(bb, slot):
        i, s_x, s_c = slot // 4, (slot // 2) % 2, slot % 2
        return s_x, (z + NZ - dz_of((bb + 15 - s_c) % 8, xl, i)) % NZ, s_c

    def slab(ref, slot):
        return ref.at[pl.ds(pl.multiple_of(slot * SLOT, SLOT), SLOT)]

    def tok_half(which):
        return tok_hbm.at[:, pl.ds(pl.multiple_of(which * HALF, 128), HALF)]

    local = [
        pltpu.make_async_copy(tok_hbm, tok, loc.at[0]),
        pltpu.make_async_copy(wg_hbm, wg.at[0], loc.at[1]),
        pltpu.make_async_copy(wu_hbm, wu.at[0], loc.at[2]),
        pltpu.make_async_copy(wd_hbm, wd.at[0], loc.at[3]),
        pltpu.make_async_copy(tok_half(xl), tq.at[pl.ds(0, NT)], loc.at[4]),
    ]
    for copy in local:
        copy.start()

    barrier = pltpu.get_barrier_semaphore()

    def greet(to):
        pl.semaphore_signal(barrier, inc=1, device_id=to, device_id_type=MESH)

    partner = (b, chip * 2 + 1 - core)
    across = dev(b, 1 - xl, z, core)
    up_z = dev(b, xl, (z + 1) % NZ, core)
    down_z = dev(b, xl, (z + NZ - 1) % NZ, core)

    @pl.loop(1, NDP)
    def _(k):
        greet(((b + k) % NDP, ex))

    for to in (partner, across, up_z, down_z):
        greet(to)

    @pl.when(active)
    def _():
        @pl.loop(0, 8)
        def _(s):
            s_x, s_z, s_c = source_of(b, s)
            greet(dev(b, s_x, s_z, s_c))

    @pl.loop(0, EXPERTS)
    def _(n):
        bb = n // 4
        to_x, to_z = dest_of(bb, n % 4)
        greet(dev(b, to_x, to_z, bb % 2))

    @pl.loop(0, NDP)
    def _(k):
        @pl.when(jnp.logical_not(own_half & (k == b)))
        def _():
            greet(dev(k, b // 4, z, core))

    row = iota((4 * SLOT, NT), 0)
    k_row = row // SLOT
    e_row = (k_row // 2) * NZ + (z + dz_of((b + 15 - core) % 8, k_row // 2, k_row % 2)) % NZ
    hit = (routes_t[0:1, :] == e_row) | (routes_t[1:2, :] == e_row)
    before = ones_where(iota((NT, NT), 0) < iota((NT, NT), 1))
    rank = dot(ones_where(hit), before)
    select = ones_where(hit & (rank == (row % SLOT).astype(F32)))
    local[0].wait()
    for n in range(D // CHUNK):
        cols = pl.ds(n * CHUNK, CHUNK)
        sbuf[:, cols] = dot(select, tok[:, cols]).astype(BF16)

    hid = iota((2 * HH, CHUNK), 0)
    lane = iota((2 * HH, CHUNK), 1)
    for h in range(2):
        here = (hid >= h * HH) & (hid < (h + 1) * HH)
        total = None
        for n, part in enumerate((dg[...], du[...], dd_t[...])):
            placed = ones_where(here & (lane == hid - h * HH + n * HH))
            term = dot(part, placed)
            total = term if total is None else total + term
        pack[h] = total.astype(BF16)

    pl.semaphore_wait(
        barrier, jnp.where(own_half, 7, 8) + 7 + 4 + 4 + EXPERTS
    )

    def dispatch(h, k):
        to_x, to_z = dest_of(b, k)
        slot = (k % 2) * 4 + xl * 2 + core
        cols = pl.ds(pl.multiple_of(h * HALF, 128), HALF)
        return remote(
            slab(sbuf, k).at[:, cols], slab(rbuf, slot).at[:, cols],
            dis_send.at[h * 4 + k], dis_recv.at[h * 8 + slot], dev(b, to_x, to_z, b % 2),
        )

    @pl.loop(0, 8)
    def _(n):
        dispatch(n // 4, n % 4).start()

    to_partner = [
        remote(pack.at[1 - core], theirs, core_send.at[0], core_recv.at[0], partner),
        remote(tok_half(xl), tq.at[pl.ds(NT, NT)], core_send.at[1], core_recv.at[1], partner),
        remote(wg_hbm, wg.at[1], core_send.at[2], core_recv.at[2], partner),
        remote(wu_hbm, wu.at[1], core_send.at[3], core_recv.at[3], partner),
        remote(wd_hbm, wd.at[1], core_send.at[4], core_recv.at[4], partner),
    ]
    for copy in to_partner:
        copy.start()
    tok_across = remote(
        tok_half(1 - xl), tq.at[pl.ds(2 * NT, NT)], ac_send.at[0], ac_recv.at[0], across
    )
    tok_across.start()

    place = iota((EXPERTS * SLOT, NT), 0)
    hit0 = routes_t[0:1, :] == place // SLOT
    hit1 = routes_t[1:2, :] == place // SLOT
    rank_all = dot(ones_where(hit0 | hit1), before)
    share = jnp.where(hit0, weights_t[0:1, :], 0.0) + jnp.where(hit1, weights_t[1:2, :], 0.0)
    share = jnp.where(rank_all == (place % SLOT).astype(F32), share, 0.0).T
    share_hi = share.astype(BF16)
    share_lo = (share - share_hi.astype(F32)).astype(BF16)

    to_partner[0].wait_recv()
    mine = pack[core]
    first = jnp.where(core == 0, mine, theirs[...])
    second = jnp.where(core == 0, theirs[...], mine)
    dense_w[pl.ds(pl.multiple_of(z * CHIP_ROWS, 16), CHIP_ROWS), :] = jnp.concatenate(
        [first, second], axis=0
    )

    slot_row = iota((BLOCK, 8 * SLOT), 0)
    squeeze = ones_where(
        iota((BLOCK, 8 * SLOT), 1) == (slot_row // CAP) * SLOT + slot_row % CAP
    )

    def x_part(yy, h):
        return xbuf.at[yy, :, pl.ds(pl.multiple_of(h * HALF, 128), HALF)]

    def spread(h, k):
        return remote(
            x_part(y, h), x_part(y, h), bc_send.at[h * 7 + k - 1], bc_recv.at[h * 4 + y],
            ((b + k) % NDP, ex),
        )

    def wait_spread(yy, h):
        remote(
            x_part(yy, h), x_part(yy, h), bc_send.at[0], bc_recv.at[h * 4 + yy], partner
        ).wait_recv()

    @pl.when(active)
    def _():
        for h in range(2):
            cols = pl.ds(h * HALF, HALF)

            @pl.loop(0, 8)
            def _(s):
                remote(
                    slab(sbuf, 0).at[:, cols], slab(rbuf, s).at[:, cols],
                    dis_send.at[0], dis_recv.at[h * 8 + s], partner,
                ).wait_recv()

            xbuf[y, :, cols] = dot(squeeze, rbuf[:, cols]).astype(BF16)

            @pl.loop(1, NDP)
            def _(k):
                spread(h, k).start()

    tok_across.wait_recv()
    relay = remote(
        tq.at[pl.ds(2 * NT, NT)], tq.at[pl.ds(3 * NT, NT)], core_send.at[5], core_recv.at[5],
        partner,
    )
    relay.start()

    @pl.when(jnp.logical_not(active))
    def _():
        wait_spread(y, 0)

    def shard(zz, p):
        return dense_w.at[
            pl.ds(pl.multiple_of(zz * CHIP_ROWS, 16), CHIP_ROWS),
            pl.ds(p * PIECE, PIECE),
        ]

    def go_right(k, p):
        s = shard((z + NZ - k) % NZ, p)
        return remote(s, s, right_send.at[2 * k + p], right_recv.at[2 * k + p], up_z)

    def go_left(k, p):
        s = shard((z + k) % NZ, p)
        return remote(s, s, left_send.at[2 * k + p], left_recv.at[2 * k + p], down_z)

    for p in range(2):
        go_right(0, p).start()
        go_left(0, p).start()
    for copy in local[1:4]:
        copy.wait()
    for copy in to_partner[2:5]:
        copy.wait_recv()

    def back(yy, to):
        return remote(
            obuf.at[yy, to], rsum.at[yy, b], rs_send.at[yy * NDP + to],
            rs_recv.at[yy * NDP + b], (to, ex),
        )

    def expert_block(yy):
        for h in range(2):
            first_half = active if h == 1 else (active | (yy == y))

            @pl.when(jnp.logical_not((yy == y) & first_half))
            def _():
                wait_spread(yy, h)

        x = xbuf[yy]
        hidden = [
            (silu(dot_nt(x, wg[h])) * dot_nt(x, wu[h])).astype(BF16) for h in range(2)
        ]
        for n in range(NDP // 2):
            cols = pl.ds(n * 2 * COLS, 2 * COLS)
            value = (dot(hidden[0], wd[0, :, cols]) + dot(hidden[1], wd[1, :, cols])).astype(BF16)
            obuf[yy, 2 * n] = value[:, 0:COLS]
            obuf[yy, 2 * n + 1] = value[:, COLS:2 * COLS]

        @pl.loop(1, NDP)
        def _(k):
            back(yy, (b + k) % NDP).start()

    @pl.loop(1, 8)
    def _(k):
        for p in range(2):
            go_right(k - 1, p).wait_recv()
            go_right(k, p).start()
            go_left(k - 1, p).wait_recv()

            @pl.when(k < 7)
            def _():
                go_left(k, p).start()

        @pl.when((k >= 3) & (k < 7))
        def _():
            expert_block(k - 3)

    for p in range(2):
        go_right(7, p).wait_recv()

    local[4].wait()
    to_partner[1].wait_recv()
    relay.wait_recv()
    both = dot(tq[...], dense_w[:, 0:384])
    gu[...] = both[0:2 * NT]
    gu_send[...] = both[2 * NT:4 * NT].astype(BF16)
    gu_across = remote(gu_send, gu_recv, ac_send.at[1], ac_recv.at[1], across)
    gu_across.start()

    widen_col = iota((8 * SLOT, BLOCK), 1)
    widen = ones_where(
        iota((8 * SLOT, BLOCK), 0) == (widen_col // CAP) * SLOT + widen_col % CAP
    )

    def give(yy, s):
        s_x, s_z, s_c = source_of(2 * yy + core, s)
        return remote(
            slab(tbuf.at[yy], s), slab(ret, chip), ret_send.at[yy * 8 + s],
            ret_recv.at[chip], dev(b, s_x, s_z, s_c),
        )

    def sum_block(yy):
        @pl.loop(1, NDP)
        def _(k):
            src = (b + k) % NDP
            remote(
                obuf.at[yy, 0], rsum.at[yy, src], rs_send.at[0],
                rs_recv.at[yy * NDP + src], partner,
            ).wait_recv()

        total = obuf[yy, b].astype(F32)
        for k in range(1, NDP):
            total = total + rsum[yy, (b + k) % NDP].astype(F32)
        tbuf[yy] = dot(widen, total.astype(BF16)).astype(BF16)

        @pl.loop(0, 8)
        def _(s):
            give(yy, s).start()

    sum_block(0)

    gu_across.wait_recv()
    both = gu[...] + gu_recv[...].astype(F32)
    dense_hidden = silu(both) * pltpu.roll(both, 384 - HH, 1)
    dense_hidden = jnp.where(iota((2 * NT, 384), 1) < HH, dense_hidden, 0.0)
    hbuf[0:2 * NT] = pltpu.roll(dense_hidden, 2 * HH - 256, 1)[:, 0:256].astype(BF16)
    h_across = remote(
        hbuf.at[pl.ds(0, 2 * NT)], hbuf.at[pl.ds(2 * NT, 2 * NT)], ac_send.at[2], ac_recv.at[2],
        across,
    )
    h_across.start()

    sum_block(1)
    sum_block(2)

    h_across.wait_recv()
    for n in range(HALF // PIECE):
        cols = pl.ds(n * PIECE, PIECE)
        part = dot_nt(hbuf[...], dense_w[n * PIECE:(n + 1) * PIECE, 256:512])
        for t in range(2):
            d_mine[t, :, cols] = part[2 * t * NT:(2 * t + 1) * NT]
            d_send[t, :, cols] = part[(2 * t + 1) * NT:(2 * t + 2) * NT].astype(BF16)
    swap = remote(d_send, d_recv, core_send.at[6], core_recv.at[6], partner)
    swap.start()

    sum_block(3)

    swap.wait_recv()

    def finish(t, q):
        to = 4 * xl + q
        to_x = (xl + t) % 2
        return remote(
            dterm.at[t, q], fin.at[b], fin_send.at[t * 4 + q], fin_recv.at[b],
            dev(to, to_x, z, core),
        )

    for t in range(2):
        for n in range(2):
            cols = pl.ds(n * 2 * COLS, 2 * COLS)
            value = (d_mine[t, :, cols] + d_recv[t, :, cols].astype(F32)).astype(BF16)
            dterm[t, 2 * n] = value[:, 0:COLS]
            dterm[t, 2 * n + 1] = value[:, COLS:2 * COLS]

    def others(t, q):
        return jnp.logical_not(own_half & (t == 0) & (4 * xl + q == b))

    @pl.loop(0, 8)
    def _(n):
        @pl.when(others(n // 4, n % 4))
        def _():
            finish(n // 4, n % 4).start()

    @pl.when(own_half)
    def _():
        fin[b] = dterm[0, b % 4]

    @pl.loop(0, EXPERTS)
    def _(e):
        remote(
            slab(tbuf.at[0], 0), slab(ret, e), ret_send.at[0], ret_recv.at[e], partner
        ).wait_recv()

    rows = ret[...]
    total = dot(share_hi, rows) + dot(share_lo, rows)

    @pl.loop(0, NDP)
    def _(k):
        @pl.when(jnp.logical_not(own_half & (k == b)))
        def _():
            remote(
                dterm.at[0, 0], fin.at[k], fin_send.at[0], fin_recv.at[k], partner
            ).wait_recv()

    for k in range(NDP):
        total = total + fin[k].astype(F32)
    out[...] = total.astype(BF16)

    for copy in to_partner:
        copy.wait_send()
    for copy in (tok_across, relay, gu_across, h_across, swap):
        copy.wait_send()

    @pl.loop(0, 8)
    def _(n):
        dispatch(n // 4, n % 4).wait_send()

        for p in range(2):
            go_right(n, p).wait_send()

            @pl.when(n < 7)
            def _():
                go_left(n, p).wait_send()

        @pl.when(others(n // 4, n % 4))
        def _():
            finish(n // 4, n % 4).wait_send()

    @pl.loop(0, EXPERTS)
    def _(n):
        give(n // 8, n % 8).wait_send()

        @pl.when(n % 8 != b)
        def _():
            back(n // 8, n % 8).wait_send()

    @pl.when(active)
    def _():
        @pl.loop(1, NDP)
        def _(k):
            spread(0, k).wait_send()
            spread(1, k).wait_send()


def per_device(
    tokens, routes, gate_weights, w_dense_gate, w_dense_up, w_dense_down,
    w_exp_gate, w_exp_up, w_exp_down,
):
    rows = w_dense_gate.shape[0]
    vmem = pl.BlockSpec(memory_space=pltpu.VMEM)
    hbm = pl.BlockSpec(memory_space=pl.ANY)
    dma = pltpu.SemaphoreType.DMA
    return pl.pallas_call(
        kernel,
        out_shape=jax.ShapeDtypeStruct((NT, COLS), BF16),
        in_specs=[vmem] * 5 + [hbm] * 4,
        out_specs=vmem,
        scratch_shapes=[
            pltpu.VMEM((NT, D), BF16),
            pltpu.VMEM((4 * NT, HALF), BF16),
            pltpu.VMEM((4 * SLOT, D), BF16),
            pltpu.VMEM((8 * SLOT, D), BF16),
            pltpu.VMEM((NY, BLOCK, D), BF16),
            pltpu.VMEM((NY, NDP, BLOCK, COLS), BF16),
            pltpu.VMEM((NY, NDP, BLOCK, COLS), BF16),
            pltpu.VMEM((NY, 8 * SLOT, COLS), BF16),
            pltpu.VMEM((EXPERTS * SLOT, COLS), BF16),
            pltpu.VMEM((2, HH, D), BF16),
            pltpu.VMEM((2, HH, D), BF16),
            pltpu.VMEM((2, HH, D), BF16),
            pltpu.VMEM((2, rows, CHUNK), BF16),
            pltpu.VMEM((rows, CHUNK), BF16),
            pltpu.VMEM((HALF, CHUNK), BF16),
            pltpu.VMEM((2 * NT, 384), F32),
            pltpu.VMEM((2 * NT, 384), BF16),
            pltpu.VMEM((2 * NT, 384), BF16),
            pltpu.VMEM((4 * NT, 256), BF16),
            pltpu.VMEM((2, NT, HALF), F32),
            pltpu.VMEM((2, NT, HALF), BF16),
            pltpu.VMEM((2, NT, HALF), BF16),
            pltpu.VMEM((2, 4, NT, COLS), BF16),
            pltpu.VMEM((NDP, NT, COLS), BF16),
            dma((5,)), dma((7,)), dma((7,)), dma((3,)), dma((3,)), dma((8,)), dma((16,)),
            dma((14,)), dma((8,)), dma((16,)), dma((16,)), dma((14,)), dma((14,)),
            dma((32,)), dma((32,)), dma((32,)), dma((32,)), dma((8,)), dma((8,)),
        ],
        compiler_params=pltpu.CompilerParams(
            collective_id=0, has_side_effects=True, vmem_limit_bytes=56 * 1024 * 1024
        ),
    )(
        routes.T, gate_weights.T, w_dense_gate, w_dense_up, w_dense_down.T, tokens,
        w_exp_gate[0, 0].T, w_exp_up[0, 0].T, w_exp_down[0, 0],
    )


def solution(mesh):
    in_specs = (
        P("expert", None),
        P("expert", None),
        P("expert", None),
        P("expert", "dp"),
        P("expert", "dp"),
        P("dp", "expert"),
        P("dp", "expert", None, None),
        P("dp", "expert", None, None),
        P("dp", "expert", None, None),
    )
    return jax.shard_map(
        per_device, mesh=mesh, in_specs=in_specs, out_specs=P("expert", "dp"), check_vma=False
    )
```

```python
import jax
import jax.numpy as jnp
from jax import lax
from jax.experimental import pallas as pl
from jax.experimental.pallas import tpu as pltpu
from jax.sharding import PartitionSpec as P

CAP = 10
SLOT = 16
NZ = 16
NY = 4
NDP = 8
NT = 128
D = 3584
HALF = D // 2
HH = 152
BLOCK = 8 * CAP
CHIP_ROWS = 112
COLS = 448
CHUNK = 512
PIECE = 256
EXPERTS = 32
MESH = pl.DeviceIdType.MESH
F32 = jnp.float32
BF16 = jnp.bfloat16


def dz_of(j, xl_to, i):
    d = jnp.where(xl_to == 0, j, 8 - j)
    edge = (d % 8) == 0
    first = jnp.where(edge, 0, d)
    second = jnp.where(edge, 8, NZ - d)
    return jnp.where(i == 0, first, second)


def iota(shape, dim):
    return lax.broadcasted_iota(jnp.int32, shape, dim)


def ones_where(mask):
    return jnp.where(mask, 1.0, 0.0).astype(BF16)


def dot(a, b):
    return jnp.dot(a, b, preferred_element_type=F32)


def dot_nt(a, b):
    return lax.dot_general(a, b, (((1,), (1,)), ((), ())), preferred_element_type=F32)


def silu(v):
    return v / (1.0 + jnp.exp(-v))


def kernel(
    routes_t, weights_t, dg, du, dd_t, tok_hbm, wg_hbm, wu_hbm, wd_hbm, out,
    tok, tq, sbuf, rbuf, xbuf, obuf, rsum, keep, cross, crossed, tbuf, ret, wg, wu, wd, pack, theirs, dense_w,
    acc, hidv, gu, gu_send, gu_recv, hbuf, d_mine, d_send, d_recv, dterm, fin,
    loc, core_send, core_recv, ac_send, ac_recv, dis_send, dis_recv, bx_send, by_send, bp_send, bc_recv,
    right_send, right_recv, left_send, left_recv,
    rs_send, rs_recv, cx_send, cx_recv, ret_send, ret_recv, fin_send, fin_recv,
):
    b = lax.axis_index("dp")
    ex = lax.axis_index("expert")
    core = ex % 2
    chip = ex // 2
    z = chip % NZ
    xl = chip // NZ
    y = b // 2
    side = b % 2
    active = side == core
    own_half = (b // 4) == xl

    def dev(bb, xx, zz, cc):
        return (bb, (xx * NZ + zz) * 2 + cc)

    def remote(src, dst, send, recv, to):
        return pltpu.make_async_remote_copy(
            src_ref=src, dst_ref=dst, send_sem=send, recv_sem=recv, device_id=to,
            device_id_type=MESH,
        )

    def dest_of(bb, k):
        to_x, i = k // 2, k % 2
        return to_x, (z + dz_of((bb + 15 - core) % 8, to_x, i)) % NZ

    def source_of(bb, slot):
        i, s_x, s_c = slot // 4, (slot // 2) % 2, slot % 2
        return s_x, (z + NZ - dz_of((bb + 15 - s_c) % 8, xl, i)) % NZ, s_c

    def slab(ref, slot):
        return ref.at[pl.ds(pl.multiple_of(slot * SLOT, SLOT), SLOT)]

    def tok_half(which):
        return tok_hbm.at[:, pl.ds(pl.multiple_of(which * HALF, 128), HALF)]

    local = [
        pltpu.make_async_copy(tok_hbm, tok, loc.at[0]),
        pltpu.make_async_copy(wg_hbm, wg.at[0], loc.at[1]),
        pltpu.make_async_copy(wu_hbm, wu.at[0], loc.at[2]),
        pltpu.make_async_copy(wd_hbm, wd.at[0], loc.at[3]),
        pltpu.make_async_copy(tok_half(xl), tq.at[pl.ds(0, NT)], loc.at[4]),
    ]
    for copy in local:
        copy.start()

    barrier = pltpu.get_barrier_semaphore()

    def greet(to):
        pl.semaphore_signal(barrier, inc=1, device_id=to, device_id_type=MESH)

    partner = (b, chip * 2 + 1 - core)
    across = dev(b, 1 - xl, z, core)
    up_z = dev(b, xl, (z + 1) % NZ, core)
    down_z = dev(b, xl, (z + NZ - 1) % NZ, core)

    def along_y(d):
        return (((y + d) % NY) * 2 + side, ex)

    across_hi = (2 * y + 1 - side, ex)
    for to in (
        along_y(1), along_y(2), along_y(3), across_hi, partner, across, up_z, down_z
    ):
        greet(to)

    @pl.when(active)
    def _():
        @pl.loop(0, 8)
        def _(s):
            s_x, s_z, s_c = source_of(b, s)
            greet(dev(b, s_x, s_z, s_c))

    @pl.loop(0, EXPERTS)
    def _(n):
        bb = n // 4
        to_x, to_z = dest_of(bb, n % 4)
        greet(dev(b, to_x, to_z, bb % 2))

    @pl.loop(0, NDP)
    def _(k):
        @pl.when(jnp.logical_not(own_half & (k == b)))
        def _():
            greet(dev(k, b // 4, z, core))

    row = iota((4 * SLOT, NT), 0)
    k_row = row // SLOT
    e_row = (k_row // 2) * NZ + (z + dz_of((b + 15 - core) % 8, k_row // 2, k_row % 2)) % NZ
    hit = (routes_t[0:1, :] == e_row) | (routes_t[1:2, :] == e_row)
    before = ones_where(iota((NT, NT), 0) < iota((NT, NT), 1))
    rank = dot(ones_where(hit), before)
    select = ones_where(hit & (rank == (row % SLOT).astype(F32)))
    local[0].wait()
    for n in range(D // CHUNK):
        cols = pl.ds(n * CHUNK, CHUNK)
        sbuf[:, cols] = dot(select, tok[:, cols]).astype(BF16)

    hid = iota((2 * HH, CHUNK), 0)
    lane = iota((2 * HH, CHUNK), 1)
    for h in range(2):
        here = (hid >= h * HH) & (hid < (h + 1) * HH)
        total = None
        for n, part in enumerate((dg[...], du[...], dd_t[...])):
            placed = ones_where(here & (lane == hid - h * HH + n * HH))
            term = dot(part, placed)
            total = term if total is None else total + term
        pack[h] = total.astype(BF16)

    pl.semaphore_wait(
        barrier, jnp.where(own_half, 7, 8) + 8 + 4 + EXPERTS
    )

    def dispatch(h, k):
        to_x, to_z = dest_of(b, k)
        slot = (k % 2) * 4 + xl * 2 + core
        cols = pl.ds(pl.multiple_of(h * HALF, 128), HALF)
        return remote(
            slab(sbuf, k).at[:, cols], slab(rbuf, slot).at[:, cols],
            dis_send.at[h * 4 + k], dis_recv.at[h * 8 + slot], dev(b, to_x, to_z, b % 2),
        )

    @pl.loop(0, 8)
    def _(n):
        dispatch(n // 4, n % 4).start()

    to_partner = [
        remote(pack.at[1 - core], theirs, core_send.at[0], core_recv.at[0], partner),
        remote(tok_half(xl), tq.at[pl.ds(NT, NT)], core_send.at[1], core_recv.at[1], partner),
        remote(wg_hbm, wg.at[1], core_send.at[2], core_recv.at[2], partner),
        remote(wu_hbm, wu.at[1], core_send.at[3], core_recv.at[3], partner),
        remote(wd_hbm, wd.at[1], core_send.at[4], core_recv.at[4], partner),
    ]
    for copy in to_partner:
        copy.start()
    tok_across = remote(
        tok_half(1 - xl), tq.at[pl.ds(2 * NT, NT)], ac_send.at[0], ac_recv.at[0], across
    )
    tok_across.start()

    place = iota((EXPERTS * SLOT, NT), 0)
    hit0 = routes_t[0:1, :] == place // SLOT
    hit1 = routes_t[1:2, :] == place // SLOT
    rank_all = dot(ones_where(hit0 | hit1), before)
    share = jnp.where(hit0, weights_t[0:1, :], 0.0) + jnp.where(hit1, weights_t[1:2, :], 0.0)
    share = jnp.where(rank_all == (place % SLOT).astype(F32), share, 0.0).T
    share_hi = share.astype(BF16)
    share_lo = (share - share_hi.astype(F32)).astype(BF16)

    to_partner[0].wait_recv()
    mine = pack[core]
    first = jnp.where(core == 0, mine, theirs[...])
    second = jnp.where(core == 0, theirs[...], mine)
    dense_w[pl.ds(pl.multiple_of(z * CHIP_ROWS, 16), CHIP_ROWS), :] = jnp.concatenate(
        [first, second], axis=0
    )

    slot_row = iota((BLOCK, 8 * SLOT), 0)
    squeeze = ones_where(
        iota((BLOCK, 8 * SLOT), 1) == (slot_row // CAP) * SLOT + slot_row % CAP
    )

    def block_rows(yy):
        return pl.ds(pl.multiple_of(yy * BLOCK, 16), BLOCK)

    def x_part(yy, h):
        return xbuf.at[block_rows(yy), pl.ds(pl.multiple_of(h * HALF, 128), HALF)]

    def wait_spread(yy, h):
        remote(
            x_part(yy, h), x_part(yy, h), bx_send.at[0], bc_recv.at[h * NY + yy], partner
        ).wait_recv()

    def spread_x(h):
        return remote(
            x_part(y, h), x_part(y, h), bx_send.at[h], bc_recv.at[h * NY + y], across_hi
        )

    def spread_y(h, n):
        return remote(
            x_part(y, h), x_part(y, h), by_send.at[2 * h + n], bc_recv.at[h * NY + y],
            along_y(1 + 2 * n),
        )

    def pass_on(h):
        yy = (y + 3 - 2 * h) % NY
        return remote(
            x_part(yy, h), x_part(yy, h), bp_send.at[h], bc_recv.at[h * NY + yy],
            along_y(1 + 2 * h),
        )

    def shard(zz, p):
        return dense_w.at[
            pl.ds(pl.multiple_of(zz * CHIP_ROWS, 16), CHIP_ROWS),
            pl.ds(p * PIECE, PIECE),
        ]

    def go_right(k, p):
        s = shard((z + NZ - k) % NZ, p)
        return remote(s, s, right_send.at[2 * k + p], right_recv.at[2 * k + p], up_z)

    def go_left(k, p):
        s = shard((z + k) % NZ, p)
        return remote(s, s, left_send.at[2 * k + p], left_recv.at[2 * k + p], down_z)

    def ring_start():
        for p in range(2):
            go_right(0, p).start()
            go_left(0, p).start()

    @pl.when(active)
    def _():
        for h in range(2):
            cols = pl.ds(h * HALF, HALF)

            @pl.loop(0, 8)
            def _(s):
                remote(
                    slab(sbuf, 0).at[:, cols], slab(rbuf, s).at[:, cols],
                    dis_send.at[0], dis_recv.at[h * 8 + s], partner,
                ).wait_recv()

            xbuf[block_rows(y), cols] = dot(squeeze, rbuf[:, cols]).astype(BF16)

            spread_x(h).start()
            for n in range(2):
                spread_y(h, n).start()

            if h == 0:
                ring_start()

    tok_across.wait_recv()
    relay = remote(
        tq.at[pl.ds(2 * NT, NT)], tq.at[pl.ds(3 * NT, NT)], core_send.at[5], core_recv.at[5],
        partner,
    )
    relay.start()

    @pl.when(jnp.logical_not(active))
    def _():
        wait_spread(y, 0)
        for n in range(2):
            spread_y(0, n).start()
        ring_start()

    for copy in local[1:4]:
        copy.wait()
    for copy in to_partner[2:5]:
        copy.wait_recv()

    def back(yy, d):
        to = (y + d) % NY
        return remote(
            obuf.at[yy, to], rsum.at[yy, y], rs_send.at[yy * NY + d], rs_recv.at[yy * NY + y],
            along_y(d),
        )

    def gate_up(h):
        cols = pl.ds(h * HALF, HALF)
        x = xbuf[:, cols]
        return [dot_nt(x, w[half, :, cols]) for half in range(2) for w in (wg, wu)]

    def experts_first():
        wait_spread((y + 1) % NY, 0)
        wait_spread((y + 2) % NY, 0)
        for n, part in enumerate(gate_up(0)):
            acc[n] = part

    def experts_second():
        wait_spread((y + 3) % NY, 1)
        wait_spread((y + 2) % NY, 1)
        parts = [acc[n] + part for n, part in enumerate(gate_up(1))]
        for half in range(2):
            hidv[half] = (silu(parts[2 * half]) * parts[2 * half + 1]).astype(BF16)

    def expert_block(yy):
        hidden = [hidv[half, yy * BLOCK:(yy + 1) * BLOCK] for half in range(2)]
        for n in range(NY):
            cols = pl.ds(n * 2 * COLS, 2 * COLS)
            obuf[yy, n] = (
                dot(hidden[0], wd[0, :, cols]) + dot(hidden[1], wd[1, :, cols])
            ).astype(BF16)

        for d in range(1, NY):
            back(yy, d).start()

    widen_col = iota((8 * SLOT, BLOCK), 1)
    widen = ones_where(
        iota((8 * SLOT, BLOCK), 0) == (widen_col // CAP) * SLOT + widen_col % CAP
    )

    def give(yy, s):
        s_x, s_z, s_c = source_of(2 * yy + core, s)
        return remote(
            slab(tbuf.at[yy], s), slab(ret, chip), ret_send.at[yy * 8 + s],
            ret_recv.at[chip], dev(b, s_x, s_z, s_c),
        )

    def sum_y(yy):
        total = obuf[yy, y].astype(F32)
        for d in range(1, NY):
            src = (y + d) % NY
            remote(
                obuf.at[yy, 0], rsum.at[yy, src], rs_send.at[0],
                rs_recv.at[yy * NY + src], partner,
            ).wait_recv()
            total = total + rsum[yy, src].astype(F32)
        low, high = total[:, 0:COLS], total[:, COLS:2 * COLS]
        keep[yy] = jnp.where(side == 0, low, high)
        cross[yy] = jnp.where(side == 0, high, low).astype(BF16)
        cross_x(yy).start()

    def cross_x(yy):
        return remote(
            cross.at[yy], crossed.at[yy], cx_send.at[yy], cx_recv.at[yy], across_hi
        )

    def sum_x(yy):
        cross_x(yy).wait_recv()
        total = keep[yy] + crossed[yy].astype(F32)
        tbuf[yy] = dot(widen, total.astype(BF16)).astype(BF16)

        @pl.loop(0, 8)
        def _(s):
            give(yy, s).start()

    @pl.loop(1, 8)
    def _(k):
        for p in range(2):
            go_right(k - 1, p).wait_recv()
            go_right(k, p).start()
            go_left(k - 1, p).wait_recv()

            @pl.when(k < 7)
            def _():
                go_left(k, p).start()

        @pl.when(k == 1)
        def _():
            wait_spread((y + 3) % NY, 0)
            pass_on(0).start()

            @pl.when(jnp.logical_not(active))
            def _():
                wait_spread(y, 1)
                for n in range(2):
                    spread_y(1, n).start()

        @pl.when(k == 3)
        def _():
            wait_spread((y + 1) % NY, 1)
            pass_on(1).start()
            experts_first()

        @pl.when(k == 5)
        def _():
            experts_second()
            for yy in range(NY):
                expert_block(yy)

        @pl.when(k == 7)
        def _():
            sum_y(0)

    for p in range(2):
        go_right(7, p).wait_recv()

    local[4].wait()
    to_partner[1].wait_recv()
    relay.wait_recv()
    both = dot(tq[...], dense_w[:, 0:384])
    gu[...] = both[0:2 * NT]
    gu_send[...] = both[2 * NT:4 * NT].astype(BF16)
    gu_across = remote(gu_send, gu_recv, ac_send.at[1], ac_recv.at[1], across)
    gu_across.start()

    sum_x(0)
    sum_y(1)

    gu_across.wait_recv()
    both = gu[...] + gu_recv[...].astype(F32)
    dense_hidden = silu(both) * pltpu.roll(both, 384 - HH, 1)
    dense_hidden = jnp.where(iota((2 * NT, 384), 1) < HH, dense_hidden, 0.0)
    hbuf[0:2 * NT] = pltpu.roll(dense_hidden, 2 * HH - 256, 1)[:, 0:256].astype(BF16)
    h_across = remote(
        hbuf.at[pl.ds(0, 2 * NT)], hbuf.at[pl.ds(2 * NT, 2 * NT)], ac_send.at[2], ac_recv.at[2],
        across,
    )
    h_across.start()

    sum_y(2)
    sum_x(1)

    h_across.wait_recv()
    for n in range(HALF // PIECE):
        cols = pl.ds(n * PIECE, PIECE)
        part = dot_nt(hbuf[...], dense_w[n * PIECE:(n + 1) * PIECE, 256:512])
        for t in range(2):
            d_mine[t, :, cols] = part[2 * t * NT:(2 * t + 1) * NT]
            d_send[t, :, cols] = part[(2 * t + 1) * NT:(2 * t + 2) * NT].astype(BF16)
    swap = remote(d_send, d_recv, core_send.at[6], core_recv.at[6], partner)
    swap.start()

    sum_y(3)
    sum_x(2)

    swap.wait_recv()

    def finish(t, q):
        to = 4 * xl + q
        to_x = (xl + t) % 2
        return remote(
            dterm.at[t, q], fin.at[b], fin_send.at[t * 4 + q], fin_recv.at[b],
            dev(to, to_x, z, core),
        )

    for t in range(2):
        for n in range(2):
            cols = pl.ds(n * 2 * COLS, 2 * COLS)
            value = (d_mine[t, :, cols] + d_recv[t, :, cols].astype(F32)).astype(BF16)
            dterm[t, 2 * n] = value[:, 0:COLS]
            dterm[t, 2 * n + 1] = value[:, COLS:2 * COLS]

    def others(t, q):
        return jnp.logical_not(own_half & (t == 0) & (4 * xl + q == b))

    @pl.loop(0, 8)
    def _(n):
        @pl.when(others(n // 4, n % 4))
        def _():
            finish(n // 4, n % 4).start()

    @pl.when(own_half)
    def _():
        fin[b] = dterm[0, b % 4]

    sum_x(3)

    @pl.loop(0, EXPERTS)
    def _(e):
        remote(
            slab(tbuf.at[0], 0), slab(ret, e), ret_send.at[0], ret_recv.at[e], partner
        ).wait_recv()

    rows = ret[...]
    total = dot(share_hi, rows) + dot(share_lo, rows)

    @pl.loop(0, NDP)
    def _(k):
        @pl.when(jnp.logical_not(own_half & (k == b)))
        def _():
            remote(
                dterm.at[0, 0], fin.at[k], fin_send.at[0], fin_recv.at[k], partner
            ).wait_recv()

    for k in range(NDP):
        total = total + fin[k].astype(F32)
    out[...] = total.astype(BF16)

    for copy in to_partner:
        copy.wait_send()
    for copy in (tok_across, relay, gu_across, h_across, swap):
        copy.wait_send()

    @pl.loop(0, 8)
    def _(n):
        dispatch(n // 4, n % 4).wait_send()

        for p in range(2):
            go_right(n, p).wait_send()

            @pl.when(n < 7)
            def _():
                go_left(n, p).wait_send()

        @pl.when(others(n // 4, n % 4))
        def _():
            finish(n // 4, n % 4).wait_send()

    @pl.loop(0, EXPERTS)
    def _(n):
        give(n // 8, n % 8).wait_send()

    @pl.loop(0, NY)
    def _(yy):
        cross_x(yy).wait_send()
        for d in range(1, NY):
            back(yy, d).wait_send()

    for h in range(2):
        pass_on(h).wait_send()
        for n in range(2):
            spread_y(h, n).wait_send()

    @pl.when(active)
    def _():
        for h in range(2):
            spread_x(h).wait_send()


def per_device(
    tokens, routes, gate_weights, w_dense_gate, w_dense_up, w_dense_down,
    w_exp_gate, w_exp_up, w_exp_down,
):
    rows = w_dense_gate.shape[0]
    vmem = pl.BlockSpec(memory_space=pltpu.VMEM)
    hbm = pl.BlockSpec(memory_space=pl.ANY)
    dma = pltpu.SemaphoreType.DMA
    return pl.pallas_call(
        kernel,
        out_shape=jax.ShapeDtypeStruct((NT, COLS), BF16),
        in_specs=[vmem] * 5 + [hbm] * 4,
        out_specs=vmem,
        scratch_shapes=[
            pltpu.VMEM((NT, D), BF16),
            pltpu.VMEM((4 * NT, HALF), BF16),
            pltpu.VMEM((4 * SLOT, D), BF16),
            pltpu.VMEM((8 * SLOT, D), BF16),
            pltpu.VMEM((NY * BLOCK, D), BF16),
            pltpu.VMEM((NY, NY, BLOCK, 2 * COLS), BF16),
            pltpu.VMEM((NY, NY, BLOCK, 2 * COLS), BF16),
            pltpu.VMEM((NY, BLOCK, COLS), F32),
            pltpu.VMEM((NY, BLOCK, COLS), BF16),
            pltpu.VMEM((NY, BLOCK, COLS), BF16),
            pltpu.VMEM((NY, 8 * SLOT, COLS), BF16),
            pltpu.VMEM((EXPERTS * SLOT, COLS), BF16),
            pltpu.VMEM((2, HH, D), BF16),
            pltpu.VMEM((2, HH, D), BF16),
            pltpu.VMEM((2, HH, D), BF16),
            pltpu.VMEM((2, rows, CHUNK), BF16),
            pltpu.VMEM((rows, CHUNK), BF16),
            pltpu.VMEM((HALF, CHUNK), BF16),
            pltpu.VMEM((4, NY * BLOCK, HH), F32),
            pltpu.VMEM((2, NY * BLOCK, HH), BF16),
            pltpu.VMEM((2 * NT, 384), F32),
            pltpu.VMEM((2 * NT, 384), BF16),
            pltpu.VMEM((2 * NT, 384), BF16),
            pltpu.VMEM((4 * NT, 256), BF16),
            pltpu.VMEM((2, NT, HALF), F32),
            pltpu.VMEM((2, NT, HALF), BF16),
            pltpu.VMEM((2, NT, HALF), BF16),
            pltpu.VMEM((2, 4, NT, COLS), BF16),
            pltpu.VMEM((NDP, NT, COLS), BF16),
            dma((5,)), dma((7,)), dma((7,)), dma((3,)), dma((3,)), dma((8,)), dma((16,)),
            dma((2,)), dma((4,)), dma((2,)), dma((8,)),
            dma((16,)), dma((16,)), dma((14,)), dma((14,)),
            dma((16,)), dma((16,)), dma((4,)), dma((4,)), dma((32,)), dma((32,)),
            dma((8,)), dma((8,)),
        ],
        compiler_params=pltpu.CompilerParams(
            collective_id=0, has_side_effects=True, vmem_limit_bytes=56 * 1024 * 1024
        ),
    )(
        routes.T, gate_weights.T, w_dense_gate, w_dense_up, w_dense_down.T, tokens,
        w_exp_gate[0, 0].T, w_exp_up[0, 0].T, w_exp_down[0, 0],
    )


def solution(mesh):
    in_specs = (
        P("expert", None),
        P("expert", None),
        P("expert", None),
        P("expert", "dp"),
        P("expert", "dp"),
        P("dp", "expert"),
        P("dp", "expert", None, None),
        P("dp", "expert", None, None),
        P("dp", "expert", None, None),
    )
    return jax.shard_map(
        per_device, mesh=mesh, in_specs=in_specs, out_specs=P("expert", "dp"), check_vma=False
    )
```

```python
import jax
import jax.numpy as jnp
from jax import lax
from jax.experimental import pallas as pl
from jax.experimental.pallas import tpu as pltpu
from jax.sharding import PartitionSpec as P

CAP = 10
TILE = 128
TILES = 14
SEND = 144
BACK = 48
NZ = 16
NY = 4
NDP = 8
NT = 128
D = 3584
HALF = D // 2
HH = 152
BLOCK = 8 * CAP
CHIP_ROWS = 112
COLS = 448
CHUNK = 512
PIECE = 256
EXPERTS = 32
MESH = pl.DeviceIdType.MESH
F32 = jnp.float32
BF16 = jnp.bfloat16


def dz_of(j, xl_to, i):
    d = jnp.where(xl_to == 0, j, 8 - j)
    edge = (d % 8) == 0
    first = jnp.where(edge, 0, d)
    second = jnp.where(edge, 8, NZ - d)
    return jnp.where(i == 0, first, second)


def iota(shape, dim):
    return lax.broadcasted_iota(jnp.int32, shape, dim)


def ones_where(mask):
    return jnp.where(mask, 1.0, 0.0).astype(BF16)


def dot(a, b):
    return jnp.dot(a, b, preferred_element_type=F32)


def dot_nt(a, b):
    return lax.dot_general(a, b, (((1,), (1,)), ((), ())), preferred_element_type=F32)


def silu(v):
    return v / (1.0 + jnp.exp(-v))


def kernel(
    routes_t, weights_t, dg, du, dd_t, tok_hbm, wg_hbm, wu_hbm, wd_hbm, out,
    tok, tq, sbuf, rbuf, squeeze, shares, xbuf, hcat, keep, cross, crossed, tbuf, ret, wg, wu, wall, pack, theirs, dense_w,
    acc, gu, gu_send, gu_recv, hbuf, d_mine, d_send, d_recv, dterm, fin,
    loc, core_send, core_recv, ac_send, ac_recv, dis_send, dis_recv, bx_send, by_send, bp_send, bc_recv,
    right_send, right_recv, left_send, left_recv,
    wa_send, wa_recv, cx_send, cx_recv, hy_send, hp_send, hy_recv, ret_send, ret_recv, fin_send, fin_recv,
):
    b = lax.axis_index("dp")
    ex = lax.axis_index("expert")
    core = ex % 2
    chip = ex // 2
    z = chip % NZ
    xl = chip // NZ
    y = b // 2
    side = b % 2
    active = side == core
    own_half = (b // 4) == xl

    def dev(bb, xx, zz, cc):
        return (bb, (xx * NZ + zz) * 2 + cc)

    def remote(src, dst, send, recv, to):
        return pltpu.make_async_remote_copy(
            src_ref=src, dst_ref=dst, send_sem=send, recv_sem=recv, device_id=to,
            device_id_type=MESH,
        )

    def dest_of(bb, k):
        to_x, i = k // 2, k % 2
        return to_x, (z + dz_of((bb + 15 - core) % 8, to_x, i)) % NZ

    def source_of(bb, slot):
        i, s_x, s_c = slot // 4, (slot // 2) % 2, slot % 2
        return s_x, (z + NZ - dz_of((bb + 15 - s_c) % 8, xl, i)) % NZ, s_c

    def rows_of(n, size):
        return pl.ds(pl.multiple_of(n * size, 16), size)

    def pair_of(yy):
        return wd_hbm.at[:, pl.ds(pl.multiple_of(yy * 2 * COLS, 128), 2 * COLS)]

    def tok_half(which):
        return tok_hbm.at[:, pl.ds(pl.multiple_of(which * HALF, 128), HALF)]

    local = [
        pltpu.make_async_copy(tok_hbm, tok, loc.at[0]),
        pltpu.make_async_copy(wg_hbm, wg.at[0], loc.at[1]),
        pltpu.make_async_copy(wu_hbm, wu.at[0], loc.at[2]),
        pltpu.make_async_copy(pair_of(y), wall.at[0, y], loc.at[3]),
        pltpu.make_async_copy(tok_half(xl), tq.at[pl.ds(0, NT)], loc.at[4]),
    ]
    for copy in local:
        copy.start()

    barrier = pltpu.get_barrier_semaphore()

    def greet(to):
        pl.semaphore_signal(barrier, inc=1, device_id=to, device_id_type=MESH)

    partner = (b, chip * 2 + 1 - core)
    across = dev(b, 1 - xl, z, core)
    up_z = dev(b, xl, (z + 1) % NZ, core)
    down_z = dev(b, xl, (z + NZ - 1) % NZ, core)

    def along_y(d):
        return (((y + d) % NY) * 2 + side, ex)

    across_hi = (2 * y + 1 - side, ex)
    for to in (partner, across, up_z, down_z):
        greet(to)

    for to in (along_y(1), along_y(2), along_y(3), across_hi):
        greet(to)

    @pl.when(active)
    def _():
        @pl.loop(0, 8)
        def _(s):
            s_x, s_z, s_c = source_of(b, s)
            greet(dev(b, s_x, s_z, s_c))

    @pl.loop(0, EXPERTS)
    def _(n):
        bb = n // 4
        to_x, to_z = dest_of(bb, n % 4)
        greet(dev(b, to_x, to_z, bb % 2))

    @pl.loop(0, NDP)
    def _(k):
        @pl.when(jnp.logical_not(own_half & (k == b)))
        def _():
            greet(dev(k, b // 4, z, core))

    row = iota((4 * SEND, NT), 0)
    k_row, at = row // SEND, row % SEND
    e_row = (k_row // 2) * NZ + (z + dz_of((b + 15 - core) % 8, k_row // 2, k_row % 2)) % NZ
    hit = (routes_t[0:1, :] == e_row) | (routes_t[1:2, :] == e_row)
    before = ones_where(iota((NT, NT), 0) < iota((NT, NT), 1))
    rank = dot(ones_where(hit), before)
    select = jnp.where(hit & (rank == (at % CAP).astype(F32)), 1.0, 0.0)
    tile_of = at // CAP

    groups = []
    for first, tiles, size in ((0, 8, 80), (8, 6, 64)):
        rows = [slice(k * SEND + first * CAP, k * SEND + first * CAP + size) for k in range(4)]
        groups.append((
            first, tiles, size,
            jnp.concatenate([select[r] for r in rows], axis=0),
            jnp.concatenate([tile_of[r] for r in rows], axis=0),
        ))

    def fill(h):
        for first, tiles, size, chosen, tile_at in groups:
            total = None
            for n in range(first, first + tiles):
                left = jnp.where(tile_at == n, chosen, 0.0).astype(BF16)
                part = dot(left, tok[:, h * HALF + n * TILE:h * HALF + (n + 1) * TILE])
                total = part if total is None else total + part
            total = total.astype(BF16)
            for k in range(4):
                start = k * SEND + first * CAP
                sbuf[h, start:start + size] = total[k * size:(k + 1) * size]

    local[0].wait()
    fill(0)

    hid = iota((2 * HH, CHUNK), 0)
    lane = iota((2 * HH, CHUNK), 1)
    for h in range(2):
        here = (hid >= h * HH) & (hid < (h + 1) * HH)
        total = None
        for n, part in enumerate((dg[...], du[...], dd_t[...])):
            placed = ones_where(here & (lane == hid - h * HH + n * HH))
            term = dot(part, placed)
            total = term if total is None else total + term
        pack[h] = total.astype(BF16)

    pl.semaphore_wait(
        barrier, jnp.where(own_half, 7, 8) + 8 + 4 + EXPERTS
    )

    def dispatch(h, k):
        to_x, to_z = dest_of(b, k)
        slot = (k % 2) * 4 + xl * 2 + core
        return remote(
            sbuf.at[h, rows_of(k, SEND)], rbuf.at[h, rows_of(slot, SEND)],
            dis_send.at[h * 4 + k], dis_recv.at[h * 8 + slot], dev(b, to_x, to_z, b % 2),
        )

    @pl.loop(0, 4)
    def _(n):
        dispatch(0, n).start()

    fill(1)

    @pl.loop(0, 4)
    def _(n):
        dispatch(1, n).start()

    def cut_to(d):
        return remote(
            pair_of((y + d) % NY), wall.at[0, y], wa_send.at[d - 1], wa_recv.at[y], along_y(d)
        )

    for d in range(1, NY):
        cut_to(d).start()

    to_partner = [
        remote(pack.at[1 - core], theirs, core_send.at[0], core_recv.at[0], partner),
        remote(tok_half(xl), tq.at[pl.ds(NT, NT)], core_send.at[1], core_recv.at[1], partner),
        remote(wg_hbm, wg.at[1], core_send.at[2], core_recv.at[2], partner),
        remote(wu_hbm, wu.at[1], core_send.at[3], core_recv.at[3], partner),
    ]
    for copy in to_partner:
        copy.start()
    tok_across = remote(
        tok_half(1 - xl), tq.at[pl.ds(2 * NT, NT)], ac_send.at[0], ac_recv.at[0], across
    )
    tok_across.start()

    place = iota((EXPERTS * BACK, NT), 0)
    hit0 = routes_t[0:1, :] == place // BACK
    hit1 = routes_t[1:2, :] == place // BACK
    rank_all = dot(ones_where(hit0 | hit1), before)
    share = jnp.where(hit0, weights_t[0:1, :], 0.0) + jnp.where(hit1, weights_t[1:2, :], 0.0)
    share = jnp.where(rank_all == ((place % BACK) % CAP).astype(F32), share, 0.0).T
    back_tile = (iota((NT, EXPERTS * BACK), 1) % BACK) // CAP
    for n in range(4):
        mine = jnp.where(back_tile == n, share, 0.0)
        mine_hi = mine.astype(BF16)
        shares[0, n * NT:(n + 1) * NT] = mine_hi
        shares[1, n * NT:(n + 1) * NT] = (mine - mine_hi.astype(F32)).astype(BF16)

    to_partner[0].wait_recv()
    mine = pack[core]
    first = jnp.where(core == 0, mine, theirs[...])
    second = jnp.where(core == 0, theirs[...], mine)
    dense_w[pl.ds(pl.multiple_of(z * CHIP_ROWS, 16), CHIP_ROWS), :] = jnp.concatenate(
        [first, second], axis=0
    )

    def block_rows(yy):
        return pl.ds(pl.multiple_of(yy * BLOCK, 16), BLOCK)

    def x_part(yy, h):
        return xbuf.at[block_rows(yy), pl.ds(pl.multiple_of(h * HALF, 128), HALF)]

    def wait_spread(yy, h):
        remote(
            x_part(yy, h), x_part(yy, h), bx_send.at[0], bc_recv.at[h * NY + yy], partner
        ).wait_recv()

    def spread_x(yy, h):
        return remote(
            x_part(yy, h), x_part(yy, h), bx_send.at[h * NY + yy], bc_recv.at[h * NY + yy],
            across_hi,
        )

    def spread_y(h, n):
        return remote(
            x_part(y, h), x_part(y, h), by_send.at[2 * h + n], bc_recv.at[h * NY + y],
            along_y(1 + 2 * n),
        )

    def pass_on(h):
        yy = (y + 3 - 2 * h) % NY
        return remote(
            x_part(yy, h), x_part(yy, h), bp_send.at[h], bc_recv.at[h * NY + yy],
            along_y(1 + 2 * h),
        )

    def shard(zz, p):
        return dense_w.at[
            pl.ds(pl.multiple_of(zz * CHIP_ROWS, 16), CHIP_ROWS),
            pl.ds(p * PIECE, PIECE),
        ]

    def go_right(k, p):
        s = shard((z + NZ - k) % NZ, p)
        return remote(s, s, right_send.at[2 * k + p], right_recv.at[2 * k + p], up_z)

    def go_left(k, p):
        s = shard((z + k) % NZ, p)
        return remote(s, s, left_send.at[2 * k + p], left_recv.at[2 * k + p], down_z)

    def ring_step(k):
        for p in range(2):
            go_right(k - 1, p).wait_recv()
            go_right(k, p).start()
            go_left(k - 1, p).wait_recv()

            @pl.when(k < 7)
            def _():
                go_left(k, p).start()

    for p in range(2):
        go_right(0, p).start()
        go_left(0, p).start()

    @pl.when(active)
    def _():
        slot_row = iota((BLOCK, 8 * SEND), 0)
        offset = iota((BLOCK, 8 * SEND), 1) - (slot_row // CAP) * SEND - slot_row % CAP
        for n in range(TILES):
            squeeze[n * BLOCK:(n + 1) * BLOCK] = ones_where(offset == n * CAP)

        for h in range(2):

            @pl.loop(0, 8)
            def _(s):
                remote(
                    sbuf.at[h, rows_of(0, SEND)], rbuf.at[h, rows_of(s, SEND)],
                    dis_send.at[0], dis_recv.at[h * 8 + s], partner,
                ).wait_recv()

            rows = dot(squeeze[...], rbuf[h]).astype(BF16)
            for n in range(TILES):
                xbuf[block_rows(y), h * HALF + n * TILE:h * HALF + (n + 1) * TILE] = rows[
                    n * BLOCK:(n + 1) * BLOCK
                ]

            spread_x(y, h).start()
            for n in range(2):
                spread_y(h, n).start()

    relay = remote(
        tq.at[pl.ds(2 * NT, NT)], tq.at[pl.ds(3 * NT, NT)], core_send.at[5], core_recv.at[5],
        partner,
    )

    @pl.when(jnp.logical_not(active))
    def _():
        ring_step(1)
        wait_spread(y, 0)
        for n in range(2):
            spread_y(0, n).start()

    for copy in local[1:4]:
        copy.wait()
    for copy in to_partner[2:4]:
        copy.wait_recv()

    wall_partner = remote(
        wall.at[0], wall.at[1], core_send.at[4], core_recv.at[4], partner
    )

    def hid_y(g, n):
        return remote(
            hcat.at[y, g], hcat.at[y, g], hy_send.at[2 * g + n], hy_recv.at[g * NY + y],
            along_y(1 + 2 * n),
        )

    def hid_pass(g):
        yy = (y + 3 - 2 * g) % NY
        return remote(
            hcat.at[yy, g], hcat.at[yy, g], hp_send.at[g], hy_recv.at[g * NY + yy],
            along_y(1 + 2 * g),
        )

    def wait_hid(yy, g):
        remote(
            hcat.at[yy, g], hcat.at[yy, g], hp_send.at[0], hy_recv.at[g * NY + yy], partner
        ).wait_recv()

    def gate_up(h):
        cols = pl.ds(h * HALF, HALF)
        x = xbuf[:, cols]
        return [dot_nt(x, w[half, :, cols]) for half in range(2) for w in (wg, wu)]

    def experts_first():
        wait_spread((y + 1) % NY, 0)
        wait_spread((y + 2) % NY, 0)
        for n, part in enumerate(gate_up(0)):
            acc[n] = part

    def experts_second():
        @pl.when(jnp.logical_not(active))
        def _():
            for d in range(NY):
                wait_spread((y + d) % NY, 1)

        parts = [acc[n] + part for n, part in enumerate(gate_up(1))]
        hidden = jnp.concatenate(
            [
                (silu(parts[2 * half]) * parts[2 * half + 1]).astype(BF16)
                for half in range(2)
            ],
            axis=1,
        )
        for g in range(2):
            hcat[y, g] = hidden[g * 2 * BLOCK:(g + 1) * 2 * BLOCK]
            for n in range(2):
                hid_y(g, n).start()

    wide_row = iota((8 * BACK, BLOCK), 0)
    wide_at = wide_row % BACK
    wide_tile = jnp.where(
        (wide_row // BACK) * CAP + wide_at % CAP == iota((8 * BACK, BLOCK), 1),
        wide_at // CAP, -1,
    )
    widen = [ones_where(wide_tile == n) for n in range(4)]

    def give(yy, s):
        s_x, s_z, s_c = source_of(2 * yy + core, s)
        return remote(
            tbuf.at[yy, rows_of(s, BACK)], ret.at[rows_of(chip, BACK)], ret_send.at[yy * 8 + s],
            ret_recv.at[chip], dev(b, s_x, s_z, s_c),
        )

    def cross_x(g):
        return remote(cross.at[g], crossed.at[g], cx_send.at[g], cx_recv.at[g], across_hi)

    def outputs(g):
        wait_hid((y + 1 + 2 * g) % NY, g)
        wait_hid((y + 2) % NY, g)
        total = None
        for yy in range(NY):
            value = hcat[yy, g]
            for half in range(2):
                part = dot(value[:, half * HH:(half + 1) * HH], wall[half, yy])
                total = part if total is None else total + part
        low, high = total[:, 0:COLS], total[:, COLS:2 * COLS]
        keep[g] = jnp.where(side == 0, low, high)
        cross[g] = jnp.where(side == 0, high, low).astype(BF16)
        cross_x(g).start()

    def finish_outputs(g):
        cross_x(g).wait_recv()
        total = keep[g] + crossed[g].astype(F32)
        total = jnp.concatenate(
            [total.astype(BF16), jnp.zeros((2 * BLOCK, 4 * TILE - COLS), BF16)], axis=1
        )
        for i in range(2):
            wide = None
            for n in range(4):
                part = dot(
                    widen[n], total[i * BLOCK:(i + 1) * BLOCK, n * TILE:(n + 1) * TILE]
                )
                wide = part if wide is None else wide + part
            tbuf[2 * g + i] = wide.astype(BF16)

            @pl.loop(0, 8)
            def _(s):
                give(2 * g + i, s).start()

    @pl.when(active)
    def _():
        ring_step(1)

    ring_step(2)

    @pl.loop(3, 8)
    def _(k):
        @pl.when((k == 3) & active)
        def _():
            wait_spread((y + 3) % NY, 0)
            pass_on(0).start()
            wait_spread((y + 1) % NY, 1)
            pass_on(1).start()
            spread_x((y + 1) % NY, 1).start()
            wait_spread((y + 3) % NY, 1)
            spread_x((y + 3) % NY, 1).start()

        ring_step(k)

        @pl.when((k == 3) & jnp.logical_not(active))
        def _():
            wait_spread((y + 3) % NY, 0)
            pass_on(0).start()

        @pl.when((k == 4) & active)
        def _():
            wait_spread((y + 2) % NY, 1)
            spread_x((y + 2) % NY, 1).start()

        @pl.when(k == jnp.where(active, 4, 5))
        def _():
            experts_first()
            experts_second()

        @pl.when(k == 6)
        def _():
            for d in range(1, NY):
                src = (y + d) % NY
                remote(
                    pair_of(0), wall.at[0, src], wa_send.at[0], wa_recv.at[src], partner
                ).wait_recv()
            wall_partner.start()
            tok_across.wait_recv()
            relay.start()

        @pl.when(k == 6)
        def _():
            wait_hid((y + 3) % NY, 0)
            hid_pass(0).start()
            wait_hid((y + 1) % NY, 1)
            hid_pass(1).start()

        @pl.when(k == 7)
        def _():
            wall_partner.wait_recv()
            outputs(0)

    for p in range(2):
        go_right(7, p).wait_recv()

    local[4].wait()
    to_partner[1].wait_recv()
    relay.wait_recv()
    both = dot(tq[...], dense_w[:, 0:384])
    gu[...] = both[0:2 * NT]
    gu_send[...] = both[2 * NT:4 * NT].astype(BF16)
    gu_across = remote(gu_send, gu_recv, ac_send.at[1], ac_recv.at[1], across)
    gu_across.start()

    outputs(1)
    finish_outputs(0)

    gu_across.wait_recv()
    both = gu[...] + gu_recv[...].astype(F32)
    dense_hidden = silu(both) * pltpu.roll(both, 384 - HH, 1)
    dense_hidden = jnp.where(iota((2 * NT, 384), 1) < HH, dense_hidden, 0.0)
    hbuf[0:2 * NT] = pltpu.roll(dense_hidden, 2 * HH - 256, 1)[:, 0:256].astype(BF16)
    h_across = remote(
        hbuf.at[pl.ds(0, 2 * NT)], hbuf.at[pl.ds(2 * NT, 2 * NT)], ac_send.at[2], ac_recv.at[2],
        across,
    )
    h_across.start()

    def dense_down(t):
        for n in range(HALF // PIECE):
            cols = pl.ds(n * PIECE, PIECE)
            part = dot_nt(
                hbuf[2 * t * NT:2 * (t + 1) * NT], dense_w[n * PIECE:(n + 1) * PIECE, 256:512]
            )
            d_mine[t, :, cols] = part[0:NT]
            d_send[t, :, cols] = part[NT:2 * NT].astype(BF16)

    swaps = [
        remote(d_send.at[t], d_recv.at[t], core_send.at[6 + t], core_recv.at[6 + t], partner)
        for t in range(2)
    ]
    dense_down(0)
    swaps[0].start()

    finish_outputs(1)

    h_across.wait_recv()
    dense_down(1)
    swaps[1].start()

    def finish(t, q):
        to = 4 * xl + q
        to_x = (xl + t) % 2
        return remote(
            dterm.at[t, q], fin.at[b], fin_send.at[t * 4 + q], fin_recv.at[b],
            dev(to, to_x, z, core),
        )

    def others(t, q):
        return jnp.logical_not(own_half & (t == 0) & (4 * xl + q == b))

    for t in range(2):
        swaps[t].wait_recv()
        for n in range(2):
            cols = pl.ds(n * 2 * COLS, 2 * COLS)
            value = (d_mine[t, :, cols] + d_recv[t, :, cols].astype(F32)).astype(BF16)
            dterm[t, 2 * n] = value[:, 0:COLS]
            dterm[t, 2 * n + 1] = value[:, COLS:2 * COLS]
            for q in (2 * n, 2 * n + 1):
                @pl.when(others(t, q))
                def _():
                    finish(t, q).start()

    @pl.when(own_half)
    def _():
        fin[b] = dterm[0, b % 4]

    @pl.loop(0, EXPERTS)
    def _(e):
        remote(
            tbuf.at[0, rows_of(0, BACK)], ret.at[rows_of(e, BACK)], ret_send.at[0],
            ret_recv.at[e], partner,
        ).wait_recv()

    rows = ret[...]
    total = dot(shares[0], rows) + dot(shares[1], rows)
    total = jnp.concatenate([total[n * NT:(n + 1) * NT] for n in range(4)], axis=1)[:, 0:COLS]

    @pl.loop(0, NDP)
    def _(k):
        @pl.when(jnp.logical_not(own_half & (k == b)))
        def _():
            remote(
                dterm.at[0, 0], fin.at[k], fin_send.at[0], fin_recv.at[k], partner
            ).wait_recv()

    for k in range(NDP):
        total = total + fin[k].astype(F32)
    out[...] = total.astype(BF16)

    for copy in to_partner:
        copy.wait_send()
    for copy in (tok_across, relay, gu_across, h_across, *swaps):
        copy.wait_send()

    @pl.loop(0, 8)
    def _(n):
        dispatch(n // 4, n % 4).wait_send()

        for p in range(2):
            go_right(n, p).wait_send()

            @pl.when(n < 7)
            def _():
                go_left(n, p).wait_send()

        @pl.when(others(n // 4, n % 4))
        def _():
            finish(n // 4, n % 4).wait_send()

    @pl.loop(0, EXPERTS)
    def _(n):
        give(n // 8, n % 8).wait_send()

    wall_partner.wait_send()

    for d in range(1, NY):
        cut_to(d).wait_send()

    for g in range(2):
        cross_x(g).wait_send()
        hid_pass(g).wait_send()
        for n in range(2):
            hid_y(g, n).wait_send()

    pass_on(0).wait_send()
    for n in range(2):
        spread_y(0, n).wait_send()

    @pl.when(active)
    def _():
        spread_x(y, 0).wait_send()
        pass_on(1).wait_send()
        for n in range(2):
            spread_y(1, n).wait_send()
        for d in range(NY):
            spread_x((y + d) % NY, 1).wait_send()


def per_device(
    tokens, routes, gate_weights, w_dense_gate, w_dense_up, w_dense_down,
    w_exp_gate, w_exp_up, w_exp_down,
):
    rows = w_dense_gate.shape[0]
    vmem = pl.BlockSpec(memory_space=pltpu.VMEM)
    hbm = pl.BlockSpec(memory_space=pl.ANY)
    dma = pltpu.SemaphoreType.DMA
    return pl.pallas_call(
        kernel,
        out_shape=jax.ShapeDtypeStruct((NT, COLS), BF16),
        in_specs=[vmem] * 5 + [hbm] * 4,
        out_specs=vmem,
        scratch_shapes=[
            pltpu.VMEM((NT, D), BF16),
            pltpu.VMEM((4 * NT, HALF), BF16),
            pltpu.VMEM((2, 4 * SEND, TILE), BF16),
            pltpu.VMEM((2, 8 * SEND, TILE), BF16),
            pltpu.VMEM((TILES * BLOCK, 8 * SEND), BF16),
            pltpu.VMEM((2, 4 * NT, EXPERTS * BACK), BF16),
            pltpu.VMEM((NY * BLOCK, D), BF16),
            pltpu.VMEM((NY, 2, 2 * BLOCK, 2 * HH), BF16),
            pltpu.VMEM((2, 2 * BLOCK, COLS), F32),
            pltpu.VMEM((2, 2 * BLOCK, COLS), BF16),
            pltpu.VMEM((2, 2 * BLOCK, COLS), BF16),
            pltpu.VMEM((NY, 8 * BACK, TILE), BF16),
            pltpu.VMEM((EXPERTS * BACK, TILE), BF16),
            pltpu.VMEM((2, HH, D), BF16),
            pltpu.VMEM((2, HH, D), BF16),
            pltpu.VMEM((2, NY, HH, 2 * COLS), BF16),
            pltpu.VMEM((2, rows, CHUNK), BF16),
            pltpu.VMEM((rows, CHUNK), BF16),
            pltpu.VMEM((HALF, CHUNK), BF16),
            pltpu.VMEM((4, NY * BLOCK, HH), F32),
            pltpu.VMEM((2 * NT, 384), F32),
            pltpu.VMEM((2 * NT, 384), BF16),
            pltpu.VMEM((2 * NT, 384), BF16),
            pltpu.VMEM((4 * NT, 256), BF16),
            pltpu.VMEM((2, NT, HALF), F32),
            pltpu.VMEM((2, NT, HALF), BF16),
            pltpu.VMEM((2, NT, HALF), BF16),
            pltpu.VMEM((2, 4, NT, COLS), BF16),
            pltpu.VMEM((NDP, NT, COLS), BF16),
            dma((5,)), dma((8,)), dma((8,)), dma((3,)), dma((3,)), dma((8,)), dma((16,)),
            dma((8,)), dma((4,)), dma((2,)), dma((8,)),
            dma((16,)), dma((16,)), dma((14,)), dma((14,)),
            dma((3,)), dma((4,)), dma((2,)), dma((2,)), dma((4,)), dma((2,)), dma((8,)),
            dma((32,)), dma((32,)),
            dma((8,)), dma((8,)),
        ],
        compiler_params=pltpu.CompilerParams(
            collective_id=0, has_side_effects=True, vmem_limit_bytes=56 * 1024 * 1024
        ),
    )(
        routes.T, gate_weights.T, w_dense_gate, w_dense_up, w_dense_down.T, tokens,
        w_exp_gate[0, 0].T, w_exp_up[0, 0].T, w_exp_down[0, 0],
    )


def solution(mesh):
    in_specs = (
        P("expert", None),
        P("expert", None),
        P("expert", None),
        P("expert", "dp"),
        P("expert", "dp"),
        P("dp", "expert"),
        P("dp", "expert", None, None),
        P("dp", "expert", None, None),
        P("dp", "expert", None, None),
    )
    return jax.shard_map(
        per_device, mesh=mesh, in_specs=in_specs, out_specs=P("expert", "dp"), check_vma=False
    )
```

```python
import jax
import jax.numpy as jnp
from jax import lax
from jax.experimental import pallas as pl
from jax.experimental.pallas import tpu as pltpu
from jax.sharding import PartitionSpec as P

CAP = 10
TILE = 128
TILES = 14
SEND = 144
BACK = 48
NZ = 16
NY = 4
NDP = 8
NT = 128
D = 3584
HALF = D // 2
HH = 152
BLOCK = 8 * CAP
CHIP_ROWS = 112
COLS = 448
CHUNK = 512
PIECE = 256
EXPERTS = 32
MESH = pl.DeviceIdType.MESH
F32 = jnp.float32
BF16 = jnp.bfloat16


def dz_of(j, xl_to, i):
    d = jnp.where(xl_to == 0, j, 8 - j)
    edge = (d % 8) == 0
    first = jnp.where(edge, 0, d)
    second = jnp.where(edge, 8, NZ - d)
    return jnp.where(i == 0, first, second)


def iota(shape, dim):
    return lax.broadcasted_iota(jnp.int32, shape, dim)


def ones_where(mask):
    return jnp.where(mask, 1.0, 0.0).astype(BF16)


def dot(a, b):
    return jnp.dot(a, b, preferred_element_type=F32)


def dot_nt(a, b):
    return lax.dot_general(a, b, (((1,), (1,)), ((), ())), preferred_element_type=F32)


def silu(v):
    return v / (1.0 + jnp.exp(-v))


def kernel(
    routes_t, weights_t, dg, du, dd_t, tok_hbm, wg_hbm, wu_hbm, wd_hbm, out,
    tok, tq, sbuf, rbuf, squeeze, shares, xbuf, hcat, keep, cross, crossed, tbuf, ret, wg, wu, wall, pack, theirs, dense_w,
    acc, gu, gu_send, gu_recv, hbuf, d_mine, d_send, d_recv, dterm, fin,
    loc, core_send, core_recv, ac_send, ac_recv, dis_send, dis_recv, bx_send, by_send, bp_send, bc_recv,
    right_send, right_recv, left_send, left_recv,
    wa_send, wa_recv, cx_send, cx_recv, hy_send, hy_recv, ret_send, ret_recv, fin_send, fin_recv,
):
    b = lax.axis_index("dp")
    ex = lax.axis_index("expert")
    core = ex % 2
    chip = ex // 2
    z = chip % NZ
    xl = chip // NZ
    y = b // 2
    side = b % 2
    active = side == core
    own_half = (b // 4) == xl

    def dev(bb, xx, zz, cc):
        return (bb, (xx * NZ + zz) * 2 + cc)

    def remote(src, dst, send, recv, to):
        return pltpu.make_async_remote_copy(
            src_ref=src, dst_ref=dst, send_sem=send, recv_sem=recv, device_id=to,
            device_id_type=MESH,
        )

    def dest_of(bb, k):
        to_x, i = k // 2, k % 2
        return to_x, (z + dz_of((bb + 15 - core) % 8, to_x, i)) % NZ

    def source_of(bb, slot):
        i, s_x, s_c = slot // 4, (slot // 2) % 2, slot % 2
        return s_x, (z + NZ - dz_of((bb + 15 - s_c) % 8, xl, i)) % NZ, s_c

    def rows_of(n, size):
        return pl.ds(pl.multiple_of(n * size, 16), size)

    def pair_of(yy):
        return wd_hbm.at[:, pl.ds(pl.multiple_of(yy * 2 * COLS, 128), 2 * COLS)]

    def tok_half(which):
        return tok_hbm.at[:, pl.ds(pl.multiple_of(which * HALF, 128), HALF)]

    local = [
        pltpu.make_async_copy(tok_hbm, tok, loc.at[0]),
        pltpu.make_async_copy(wg_hbm, wg.at[0], loc.at[1]),
        pltpu.make_async_copy(wu_hbm, wu.at[0], loc.at[2]),
        pltpu.make_async_copy(pair_of(y), wall.at[0, y], loc.at[3]),
        pltpu.make_async_copy(tok_half(xl), tq.at[pl.ds(0, NT)], loc.at[4]),
    ]
    for copy in local:
        copy.start()

    barrier = pltpu.get_barrier_semaphore()

    def greet(to):
        pl.semaphore_signal(barrier, inc=1, device_id=to, device_id_type=MESH)

    partner = (b, chip * 2 + 1 - core)
    across = dev(b, 1 - xl, z, core)
    up_z = dev(b, xl, (z + 1) % NZ, core)
    down_z = dev(b, xl, (z + NZ - 1) % NZ, core)

    def along_y(d):
        return (((y + d) % NY) * 2 + side, ex)

    across_hi = (2 * y + 1 - side, ex)
    for to in (partner, across, up_z, down_z):
        greet(to)

    for to in (along_y(1), along_y(2), along_y(3), across_hi):
        greet(to)

    @pl.when(active)
    def _():
        @pl.loop(0, 8)
        def _(s):
            s_x, s_z, s_c = source_of(b, s)
            greet(dev(b, s_x, s_z, s_c))

    @pl.loop(0, EXPERTS)
    def _(n):
        bb = n // 4
        to_x, to_z = dest_of(bb, n % 4)
        greet(dev(b, to_x, to_z, bb % 2))

    @pl.loop(0, NDP)
    def _(k):
        @pl.when(jnp.logical_not(own_half & (k == b)))
        def _():
            greet(dev(k, b // 4, z, core))

    row = iota((4 * SEND, NT), 0)
    k_row, at = row // SEND, row % SEND
    e_row = (k_row // 2) * NZ + (z + dz_of((b + 15 - core) % 8, k_row // 2, k_row % 2)) % NZ
    hit = (routes_t[0:1, :] == e_row) | (routes_t[1:2, :] == e_row)
    before = ones_where(iota((NT, NT), 0) < iota((NT, NT), 1))
    rank = dot(ones_where(hit), before)
    select = jnp.where(hit & (rank == (at % CAP).astype(F32)), 1.0, 0.0)
    tile_of = at // CAP

    groups = []
    for first, tiles, size in ((0, 8, 80), (8, 6, 64)):
        rows = [slice(k * SEND + first * CAP, k * SEND + first * CAP + size) for k in range(4)]
        groups.append((
            first, tiles, size,
            jnp.concatenate([select[r] for r in rows], axis=0),
            jnp.concatenate([tile_of[r] for r in rows], axis=0),
        ))

    def fill(h):
        for first, tiles, size, chosen, tile_at in groups:
            total = None
            for n in range(first, first + tiles):
                left = jnp.where(tile_at == n, chosen, 0.0).astype(BF16)
                part = dot(left, tok[:, h * HALF + n * TILE:h * HALF + (n + 1) * TILE])
                total = part if total is None else total + part
            total = total.astype(BF16)
            for k in range(4):
                start = k * SEND + first * CAP
                sbuf[h, start:start + size] = total[k * size:(k + 1) * size]

    local[0].wait()
    fill(0)

    hid = iota((2 * HH, CHUNK), 0)
    lane = iota((2 * HH, CHUNK), 1)
    for h in range(2):
        here = (hid >= h * HH) & (hid < (h + 1) * HH)
        total = None
        for n, part in enumerate((dg[...], du[...], dd_t[...])):
            placed = ones_where(here & (lane == hid - h * HH + n * HH))
            term = dot(part, placed)
            total = term if total is None else total + term
        pack[h] = total.astype(BF16)

    pl.semaphore_wait(
        barrier, jnp.where(own_half, 7, 8) + 8 + 4 + EXPERTS
    )

    def dispatch(h, k):
        to_x, to_z = dest_of(b, k)
        slot = (k % 2) * 4 + xl * 2 + core
        return remote(
            sbuf.at[h, rows_of(k, SEND)], rbuf.at[h, rows_of(slot, SEND)],
            dis_send.at[h * 4 + k], dis_recv.at[h * 8 + slot], dev(b, to_x, to_z, b % 2),
        )

    @pl.loop(0, 4)
    def _(n):
        dispatch(0, n).start()

    fill(1)

    @pl.loop(0, 4)
    def _(n):
        dispatch(1, n).start()

    def cut_to(d):
        return remote(
            pair_of((y + d) % NY), wall.at[0, y], wa_send.at[d - 1], wa_recv.at[y], along_y(d)
        )

    for d in range(1, NY):
        cut_to(d).start()

    to_partner = [
        remote(pack.at[1 - core], theirs, core_send.at[0], core_recv.at[0], partner),
        remote(tok_half(xl), tq.at[pl.ds(NT, NT)], core_send.at[1], core_recv.at[1], partner),
        remote(wg_hbm, wg.at[1], core_send.at[2], core_recv.at[2], partner),
        remote(wu_hbm, wu.at[1], core_send.at[3], core_recv.at[3], partner),
    ]
    for copy in to_partner:
        copy.start()
    tok_across = remote(
        tok_half(1 - xl), tq.at[pl.ds(2 * NT, NT)], ac_send.at[0], ac_recv.at[0], across
    )
    tok_across.start()

    place = iota((EXPERTS * BACK, NT), 0)
    hit0 = routes_t[0:1, :] == place // BACK
    hit1 = routes_t[1:2, :] == place // BACK
    rank_all = dot(ones_where(hit0 | hit1), before)
    share = jnp.where(hit0, weights_t[0:1, :], 0.0) + jnp.where(hit1, weights_t[1:2, :], 0.0)
    share = jnp.where(rank_all == ((place % BACK) % CAP).astype(F32), share, 0.0).T
    back_tile = (iota((NT, EXPERTS * BACK), 1) % BACK) // CAP
    for n in range(4):
        mine = jnp.where(back_tile == n, share, 0.0)
        mine_hi = mine.astype(BF16)
        shares[0, n * NT:(n + 1) * NT] = mine_hi
        shares[1, n * NT:(n + 1) * NT] = (mine - mine_hi.astype(F32)).astype(BF16)

    to_partner[0].wait_recv()
    mine = pack[core]
    first = jnp.where(core == 0, mine, theirs[...])
    second = jnp.where(core == 0, theirs[...], mine)
    dense_w[pl.ds(pl.multiple_of(z * CHIP_ROWS, 16), CHIP_ROWS), :] = jnp.concatenate(
        [first, second], axis=0
    )

    def block_rows(yy):
        return pl.ds(pl.multiple_of(yy * BLOCK, 16), BLOCK)

    def x_part(yy, h):
        return xbuf.at[block_rows(yy), pl.ds(pl.multiple_of(h * HALF, 128), HALF)]

    def wait_spread(yy, h):
        remote(
            x_part(yy, h), x_part(yy, h), bx_send.at[0], bc_recv.at[h * NY + yy], partner
        ).wait_recv()

    def spread_x(yy, h):
        return remote(
            x_part(yy, h), x_part(yy, h), bx_send.at[h * NY + yy], bc_recv.at[h * NY + yy],
            across_hi,
        )

    def spread_y(h, n):
        return remote(
            x_part(y, h), x_part(y, h), by_send.at[3 * h + n], bc_recv.at[h * NY + y],
            along_y((1, 3, 2)[n]),
        )

    def pass_on(h):
        yy = (y + 3 - 2 * h) % NY
        return remote(
            x_part(yy, h), x_part(yy, h), bp_send.at[h], bc_recv.at[h * NY + yy],
            along_y(1 + 2 * h),
        )

    def shard(zz, p):
        return dense_w.at[
            pl.ds(pl.multiple_of(zz * CHIP_ROWS, 16), CHIP_ROWS),
            pl.ds(p * PIECE, PIECE),
        ]

    def go_right(k, p):
        s = shard((z + NZ - k) % NZ, p)
        return remote(s, s, right_send.at[2 * k + p], right_recv.at[2 * k + p], up_z)

    def go_left(k, p):
        s = shard((z + k) % NZ, p)
        return remote(s, s, left_send.at[2 * k + p], left_recv.at[2 * k + p], down_z)

    def ring_step(k):
        for p in range(2):
            go_right(k - 1, p).wait_recv()
            go_right(k, p).start()
            go_left(k - 1, p).wait_recv()

            @pl.when(k < 7)
            def _():
                go_left(k, p).start()

    for p in range(2):
        go_right(0, p).start()
        go_left(0, p).start()

    @pl.when(active)
    def _():
        slot_row = iota((BLOCK, 8 * SEND), 0)
        offset = iota((BLOCK, 8 * SEND), 1) - (slot_row // CAP) * SEND - slot_row % CAP
        for n in range(TILES):
            squeeze[n * BLOCK:(n + 1) * BLOCK] = ones_where(offset == n * CAP)

        for h in range(2):

            @pl.loop(0, 8)
            def _(s):
                remote(
                    sbuf.at[h, rows_of(0, SEND)], rbuf.at[h, rows_of(s, SEND)],
                    dis_send.at[0], dis_recv.at[h * 8 + s], partner,
                ).wait_recv()

            rows = dot(squeeze[...], rbuf[h]).astype(BF16)
            for n in range(TILES):
                xbuf[block_rows(y), h * HALF + n * TILE:h * HALF + (n + 1) * TILE] = rows[
                    n * BLOCK:(n + 1) * BLOCK
                ]

            spread_x(y, h).start()
            for n in range(2 + h):
                spread_y(h, n).start()

    relay = remote(
        tq.at[pl.ds(2 * NT, NT)], tq.at[pl.ds(3 * NT, NT)], core_send.at[5], core_recv.at[5],
        partner,
    )

    @pl.when(jnp.logical_not(active))
    def _():
        ring_step(1)
        wait_spread(y, 0)
        for n in range(2):
            spread_y(0, n).start()

    for copy in local[1:4]:
        copy.wait()
    for copy in to_partner[2:4]:
        copy.wait_recv()

    wall_partner = remote(
        wall.at[0], wall.at[1], core_send.at[4], core_recv.at[4], partner
    )

    def hid_y(g, d):
        return remote(
            hcat.at[y, g], hcat.at[y, g], hy_send.at[3 * g + d - 1], hy_recv.at[g * NY + y],
            along_y(d),
        )

    def wait_hid(yy, g):
        remote(
            hcat.at[yy, g], hcat.at[yy, g], hy_send.at[0], hy_recv.at[g * NY + yy], partner
        ).wait_recv()

    def gate_up(h):
        cols = pl.ds(h * HALF, HALF)
        x = xbuf[:, cols]
        return [dot_nt(x, w[half, :, cols]) for half in range(2) for w in (wg, wu)]

    def experts_first():
        wait_spread((y + 1) % NY, 0)
        wait_spread((y + 2) % NY, 0)
        for n, part in enumerate(gate_up(0)):
            acc[n] = part

    def experts_second():
        @pl.when(jnp.logical_not(active))
        def _():
            for d in range(NY):
                wait_spread((y + d) % NY, 1)

        parts = [acc[n] + part for n, part in enumerate(gate_up(1))]
        hidden = jnp.concatenate(
            [
                (silu(parts[2 * half]) * parts[2 * half + 1]).astype(BF16)
                for half in range(2)
            ],
            axis=1,
        )
        for g in range(2):
            hcat[y, g] = hidden[g * 2 * BLOCK:(g + 1) * 2 * BLOCK]
            for d in range(1, NY):
                hid_y(g, d).start()

    wide_row = iota((8 * BACK, BLOCK), 0)
    wide_at = wide_row % BACK
    wide_tile = jnp.where(
        (wide_row // BACK) * CAP + wide_at % CAP == iota((8 * BACK, BLOCK), 1),
        wide_at // CAP, -1,
    )
    widen = [ones_where(wide_tile == n) for n in range(4)]

    def give(yy, s):
        s_x, s_z, s_c = source_of(2 * yy + core, s)
        return remote(
            tbuf.at[yy, rows_of(s, BACK)], ret.at[rows_of(chip, BACK)], ret_send.at[yy * 8 + s],
            ret_recv.at[chip], dev(b, s_x, s_z, s_c),
        )

    def cross_x(g):
        return remote(cross.at[g], crossed.at[g], cx_send.at[g], cx_recv.at[g], across_hi)

    def outputs(g):
        for d in range(1, NY):
            wait_hid((y + d) % NY, g)
        total = None
        for yy in range(NY):
            value = hcat[yy, g]
            for half in range(2):
                part = dot(value[:, half * HH:(half + 1) * HH], wall[half, yy])
                total = part if total is None else total + part
        low, high = total[:, 0:COLS], total[:, COLS:2 * COLS]
        keep[g] = jnp.where(side == 0, low, high)
        cross[g] = jnp.where(side == 0, high, low).astype(BF16)
        cross_x(g).start()

    def finish_outputs(g):
        cross_x(g).wait_recv()
        total = keep[g] + crossed[g].astype(F32)
        total = jnp.concatenate(
            [total.astype(BF16), jnp.zeros((2 * BLOCK, 4 * TILE - COLS), BF16)], axis=1
        )
        for i in range(2):
            wide = None
            for n in range(4):
                part = dot(
                    widen[n], total[i * BLOCK:(i + 1) * BLOCK, n * TILE:(n + 1) * TILE]
                )
                wide = part if wide is None else wide + part
            tbuf[2 * g + i] = wide.astype(BF16)

            @pl.loop(0, 8)
            def _(s):
                give(2 * g + i, s).start()

    @pl.when(active)
    def _():
        ring_step(1)

    ring_step(2)

    @pl.loop(3, 8)
    def _(k):
        @pl.when((k == 3) & active)
        def _():
            wait_spread((y + 3) % NY, 0)
            pass_on(0).start()
            wait_spread((y + 1) % NY, 1)
            spread_x((y + 1) % NY, 1).start()
            wait_spread((y + 3) % NY, 1)
            spread_x((y + 3) % NY, 1).start()

        ring_step(k)

        @pl.when((k == 3) & jnp.logical_not(active))
        def _():
            wait_spread((y + 3) % NY, 0)
            pass_on(0).start()

        @pl.when((k == 4) & active)
        def _():
            wait_spread((y + 2) % NY, 1)
            spread_x((y + 2) % NY, 1).start()

        @pl.when(k == jnp.where(active, 5, 6))
        def _():
            experts_first()
            experts_second()

        @pl.when(k == 6)
        def _():
            for d in range(1, NY):
                src = (y + d) % NY
                remote(
                    pair_of(0), wall.at[0, src], wa_send.at[0], wa_recv.at[src], partner
                ).wait_recv()
            wall_partner.start()
            tok_across.wait_recv()
            relay.start()

    for p in range(2):
        go_right(7, p).wait_recv()

    local[4].wait()
    to_partner[1].wait_recv()
    relay.wait_recv()
    both = dot(tq[...], dense_w[:, 0:384])
    gu[...] = both[0:2 * NT]
    gu_send[...] = both[2 * NT:4 * NT].astype(BF16)
    gu_across = remote(gu_send, gu_recv, ac_send.at[1], ac_recv.at[1], across)
    gu_across.start()

    wall_partner.wait_recv()
    outputs(0)
    outputs(1)

    gu_across.wait_recv()
    both = gu[...] + gu_recv[...].astype(F32)
    dense_hidden = silu(both) * pltpu.roll(both, 384 - HH, 1)
    dense_hidden = jnp.where(iota((2 * NT, 384), 1) < HH, dense_hidden, 0.0)
    hbuf[0:2 * NT] = pltpu.roll(dense_hidden, 2 * HH - 256, 1)[:, 0:256].astype(BF16)
    h_across = remote(
        hbuf.at[pl.ds(0, 2 * NT)], hbuf.at[pl.ds(2 * NT, 2 * NT)], ac_send.at[2], ac_recv.at[2],
        across,
    )
    h_across.start()

    def dense_down(t):
        for n in range(HALF // PIECE):
            cols = pl.ds(n * PIECE, PIECE)
            part = dot_nt(
                hbuf[2 * t * NT:2 * (t + 1) * NT], dense_w[n * PIECE:(n + 1) * PIECE, 256:512]
            )
            d_mine[t, :, cols] = part[0:NT]
            d_send[t, :, cols] = part[NT:2 * NT].astype(BF16)

    swaps = [
        remote(d_send.at[t], d_recv.at[t], core_send.at[6 + t], core_recv.at[6 + t], partner)
        for t in range(2)
    ]
    def finish(t, q):
        to = 4 * xl + q
        to_x = (xl + t) % 2
        return remote(
            dterm.at[t, q], fin.at[b], fin_send.at[t * 4 + q], fin_recv.at[b],
            dev(to, to_x, z, core),
        )

    def others(t, q):
        return jnp.logical_not(own_half & (t == 0) & (4 * xl + q == b))

    def dense_out(t):
        swaps[t].wait_recv()
        for n in range(2):
            cols = pl.ds(n * 2 * COLS, 2 * COLS)
            value = (d_mine[t, :, cols] + d_recv[t, :, cols].astype(F32)).astype(BF16)
            dterm[t, 2 * n] = value[:, 0:COLS]
            dterm[t, 2 * n + 1] = value[:, COLS:2 * COLS]
            for q in (2 * n, 2 * n + 1):
                @pl.when(others(t, q))
                def _():
                    finish(t, q).start()

    dense_down(0)
    swaps[0].start()
    finish_outputs(0)
    dense_out(0)
    finish_outputs(1)
    h_across.wait_recv()
    dense_down(1)
    swaps[1].start()
    dense_out(1)

    @pl.when(own_half)
    def _():
        fin[b] = dterm[0, b % 4]

    for copy in to_partner:
        copy.wait_send()
    for copy in (tok_across, relay, gu_across, h_across, *swaps):
        copy.wait_send()

    @pl.loop(0, 8)
    def _(n):
        dispatch(n // 4, n % 4).wait_send()

        for p in range(2):
            go_right(n, p).wait_send()

            @pl.when(n < 7)
            def _():
                go_left(n, p).wait_send()

    wall_partner.wait_send()

    for d in range(1, NY):
        cut_to(d).wait_send()

    for g in range(2):
        cross_x(g).wait_send()
        for d in range(1, NY):
            hid_y(g, d).wait_send()

    pass_on(0).wait_send()
    for n in range(2):
        spread_y(0, n).wait_send()

    @pl.when(active)
    def _():
        spread_x(y, 0).wait_send()
        for n in range(3):
            spread_y(1, n).wait_send()
        for d in range(NY):
            spread_x((y + d) % NY, 1).wait_send()

    @pl.loop(0, EXPERTS)
    def _(e):
        remote(
            tbuf.at[0, rows_of(0, BACK)], ret.at[rows_of(e, BACK)], ret_send.at[0],
            ret_recv.at[e], partner,
        ).wait_recv()

    rows = ret[...]
    total = dot(shares[0], rows) + dot(shares[1], rows)
    total = jnp.concatenate([total[n * NT:(n + 1) * NT] for n in range(4)], axis=1)[:, 0:COLS]

    @pl.loop(0, NDP)
    def _(k):
        @pl.when(jnp.logical_not(own_half & (k == b)))
        def _():
            remote(
                dterm.at[0, 0], fin.at[k], fin_send.at[0], fin_recv.at[k], partner
            ).wait_recv()

    for k in range(NDP):
        total = total + fin[k].astype(F32)
    out[...] = total.T.astype(BF16)

    @pl.loop(0, 8)
    def _(n):
        @pl.when(others(n // 4, n % 4))
        def _():
            finish(n // 4, n % 4).wait_send()

    @pl.loop(0, EXPERTS)
    def _(n):
        give(n // 8, n % 8).wait_send()


def per_device(
    tokens, routes, gate_weights, w_dense_gate, w_dense_up, w_dense_down,
    w_exp_gate, w_exp_up, w_exp_down,
):
    rows = w_dense_gate.shape[0]
    vmem = pl.BlockSpec(memory_space=pltpu.VMEM)
    hbm = pl.BlockSpec(memory_space=pl.ANY)
    dma = pltpu.SemaphoreType.DMA
    out_t = pl.pallas_call(
        kernel,
        out_shape=jax.ShapeDtypeStruct((COLS, NT), BF16),
        in_specs=[vmem] * 5 + [hbm] * 4,
        out_specs=vmem,
        scratch_shapes=[
            pltpu.VMEM((NT, D), BF16),
            pltpu.VMEM((4 * NT, HALF), BF16),
            pltpu.VMEM((2, 4 * SEND, TILE), BF16),
            pltpu.VMEM((2, 8 * SEND, TILE), BF16),
            pltpu.VMEM((TILES * BLOCK, 8 * SEND), BF16),
            pltpu.VMEM((2, 4 * NT, EXPERTS * BACK), BF16),
            pltpu.VMEM((NY * BLOCK, D), BF16),
            pltpu.VMEM((NY, 2, 2 * BLOCK, 2 * HH), BF16),
            pltpu.VMEM((2, 2 * BLOCK, COLS), F32),
            pltpu.VMEM((2, 2 * BLOCK, COLS), BF16),
            pltpu.VMEM((2, 2 * BLOCK, COLS), BF16),
            pltpu.VMEM((NY, 8 * BACK, TILE), BF16),
            pltpu.VMEM((EXPERTS * BACK, TILE), BF16),
            pltpu.VMEM((2, HH, D), BF16),
            pltpu.VMEM((2, HH, D), BF16),
            pltpu.VMEM((2, NY, HH, 2 * COLS), BF16),
            pltpu.VMEM((2, rows, CHUNK), BF16),
            pltpu.VMEM((rows, CHUNK), BF16),
            pltpu.VMEM((HALF, CHUNK), BF16),
            pltpu.VMEM((4, NY * BLOCK, HH), F32),
            pltpu.VMEM((2 * NT, 384), F32),
            pltpu.VMEM((2 * NT, 384), BF16),
            pltpu.VMEM((2 * NT, 384), BF16),
            pltpu.VMEM((4 * NT, 256), BF16),
            pltpu.VMEM((2, NT, HALF), F32),
            pltpu.VMEM((2, NT, HALF), BF16),
            pltpu.VMEM((2, NT, HALF), BF16),
            pltpu.VMEM((2, 4, NT, COLS), BF16),
            pltpu.VMEM((NDP, NT, COLS), BF16),
            dma((5,)), dma((8,)), dma((8,)), dma((3,)), dma((3,)), dma((8,)), dma((16,)),
            dma((8,)), dma((6,)), dma((2,)), dma((8,)),
            dma((16,)), dma((16,)), dma((14,)), dma((14,)),
            dma((3,)), dma((4,)), dma((2,)), dma((2,)), dma((6,)), dma((8,)),
            dma((32,)), dma((32,)),
            dma((8,)), dma((8,)),
        ],
        compiler_params=pltpu.CompilerParams(
            collective_id=0, has_side_effects=True, vmem_limit_bytes=56 * 1024 * 1024
        ),
    )(
        routes.T, gate_weights.T, w_dense_gate, w_dense_up, w_dense_down.T, tokens,
        w_exp_gate[0, 0].T, w_exp_up[0, 0].T, w_exp_down[0, 0],
    )
    return out_t.T


def solution(mesh):
    in_specs = (
        P("expert", None),
        P("expert", None),
        P("expert", None),
        P("expert", "dp"),
        P("expert", "dp"),
        P("dp", "expert"),
        P("dp", "expert", None, None),
        P("dp", "expert", None, None),
        P("dp", "expert", None, None),
    )
    return jax.shard_map(
        per_device, mesh=mesh, in_specs=in_specs, out_specs=P("expert", "dp"), check_vma=False
    )
```

```python
import jax
import jax.numpy as jnp
from jax import lax
from jax.experimental import pallas as pl
from jax.experimental.pallas import tpu as pltpu
from jax.sharding import PartitionSpec as P

CAP = 10
TILE = 128
TILES = 14
SEND = 144
BACK = 48
NZ = 16
NY = 4
NDP = 8
NT = 128
D = 3584
HALF = D // 2
HH = 152
BLOCK = 8 * CAP
CHIP_ROWS = 112
COLS = 448
CHUNK = 512
PIECE = 256
EXPERTS = 32
MESH = pl.DeviceIdType.MESH
F32 = jnp.float32
BF16 = jnp.bfloat16


def dz_of(j, xl_to, i):
    d = jnp.where(xl_to == 0, j, 8 - j)
    edge = (d % 8) == 0
    first = jnp.where(edge, 0, d)
    second = jnp.where(edge, 8, NZ - d)
    return jnp.where(i == 0, first, second)


def iota(shape, dim):
    return lax.broadcasted_iota(jnp.int32, shape, dim)


def ones_where(mask):
    return jnp.where(mask, 1.0, 0.0).astype(BF16)


def dot(a, b):
    return jnp.dot(a, b, preferred_element_type=F32)


def dot_nt(a, b):
    return lax.dot_general(a, b, (((1,), (1,)), ((), ())), preferred_element_type=F32)


def silu(v):
    return v / (1.0 + jnp.exp(-v))


def kernel(
    routes_t, weights_t, dg, du, dd_t, tok_hbm, wg_hbm, wu_hbm, wd_hbm, out,
    tok, tq, sbuf, rbuf, squeeze, shares, xbuf, hcat, keep, cross, crossed, tbuf, ret, wg, wu, wall, pack, theirs, dense_w,
    acc, gu, gu_send, gu_recv, hbuf, d_mine, d_send, d_recv, dterm, fin,
    loc, core_send, core_recv, ac_send, ac_recv, dis_send, dis_recv, bx_send, by_send, bp_send, bc_recv,
    right_send, right_recv, left_send, left_recv,
    wa_send, wa_recv, cx_send, cx_recv, hy_send, hy_recv, ret_send, ret_recv, fin_send, fin_recv,
):
    b = lax.axis_index("dp")
    ex = lax.axis_index("expert")
    core = ex % 2
    chip = ex // 2
    z = chip % NZ
    xl = chip // NZ
    y = b // 2
    side = b % 2
    active = side == core
    own_half = (b // 4) == xl

    def dev(bb, xx, zz, cc):
        return (bb, (xx * NZ + zz) * 2 + cc)

    def remote(src, dst, send, recv, to):
        return pltpu.make_async_remote_copy(
            src_ref=src, dst_ref=dst, send_sem=send, recv_sem=recv, device_id=to,
            device_id_type=MESH,
        )

    def dest_of(bb, k):
        to_x, i = k // 2, k % 2
        return to_x, (z + dz_of((bb + 15 - core) % 8, to_x, i)) % NZ

    def source_of(bb, slot):
        i, s_x, s_c = slot // 4, (slot // 2) % 2, slot % 2
        return s_x, (z + NZ - dz_of((bb + 15 - s_c) % 8, xl, i)) % NZ, s_c

    def rows_of(n, size):
        return pl.ds(pl.multiple_of(n * size, 16), size)

    def pair_of(yy):
        return wd_hbm.at[:, pl.ds(pl.multiple_of(yy * 2 * COLS, 128), 2 * COLS)]

    def tok_half(which):
        return tok_hbm.at[:, pl.ds(pl.multiple_of(which * HALF, 128), HALF)]

    local = [
        pltpu.make_async_copy(tok_hbm, tok, loc.at[0]),
        pltpu.make_async_copy(wg_hbm, wg.at[0], loc.at[1]),
        pltpu.make_async_copy(wu_hbm, wu.at[0], loc.at[2]),
        pltpu.make_async_copy(pair_of(y), wall.at[0, y], loc.at[3]),
        pltpu.make_async_copy(tok_half(xl), tq.at[pl.ds(0, NT)], loc.at[4]),
    ]
    for copy in local:
        copy.start()

    barrier = pltpu.get_barrier_semaphore()

    def greet(to):
        pl.semaphore_signal(barrier, inc=1, device_id=to, device_id_type=MESH)

    partner = (b, chip * 2 + 1 - core)
    across = dev(b, 1 - xl, z, core)
    up_z = dev(b, xl, (z + 1) % NZ, core)
    down_z = dev(b, xl, (z + NZ - 1) % NZ, core)

    def along_y(d):
        return (((y + d) % NY) * 2 + side, ex)

    across_hi = (2 * y + 1 - side, ex)
    for to in (partner, across, up_z, down_z):
        greet(to)

    for to in (along_y(1), along_y(2), along_y(3), across_hi):
        greet(to)

    @pl.when(active)
    def _():
        @pl.loop(0, 8)
        def _(s):
            s_x, s_z, s_c = source_of(b, s)
            greet(dev(b, s_x, s_z, s_c))

    @pl.loop(0, EXPERTS)
    def _(n):
        bb = n // 4
        to_x, to_z = dest_of(bb, n % 4)
        greet(dev(b, to_x, to_z, bb % 2))

    @pl.loop(0, NDP)
    def _(k):
        @pl.when(jnp.logical_not(own_half & (k == b)))
        def _():
            greet(dev(k, b // 4, z, core))

    row = iota((4 * SEND, NT), 0)
    k_row, at = row // SEND, row % SEND
    e_row = (k_row // 2) * NZ + (z + dz_of((b + 15 - core) % 8, k_row // 2, k_row % 2)) % NZ
    hit = (routes_t[0:1, :] == e_row) | (routes_t[1:2, :] == e_row)
    before = ones_where(iota((NT, NT), 0) < iota((NT, NT), 1))
    rank = dot(ones_where(hit), before)
    select = jnp.where(hit & (rank == (at % CAP).astype(F32)), 1.0, 0.0)
    tile_of = at // CAP

    groups = []
    for first, tiles, size in ((0, 8, 80), (8, 6, 64)):
        rows = [slice(k * SEND + first * CAP, k * SEND + first * CAP + size) for k in range(4)]
        groups.append((
            first, tiles, size,
            jnp.concatenate([select[r] for r in rows], axis=0),
            jnp.concatenate([tile_of[r] for r in rows], axis=0),
        ))

    def fill(h):
        for first, tiles, size, chosen, tile_at in groups:
            total = None
            for n in range(first, first + tiles):
                left = jnp.where(tile_at == n, chosen, 0.0).astype(BF16)
                part = dot(left, tok[:, h * HALF + n * TILE:h * HALF + (n + 1) * TILE])
                total = part if total is None else total + part
            total = total.astype(BF16)
            for k in range(4):
                start = k * SEND + first * CAP
                sbuf[h, start:start + size] = total[k * size:(k + 1) * size]

    local[0].wait()
    fill(0)

    hid = iota((2 * HH, CHUNK), 0)
    lane = iota((2 * HH, CHUNK), 1)
    for h in range(2):
        here = (hid >= h * HH) & (hid < (h + 1) * HH)
        total = None
        for n, part in enumerate((dg[...], du[...], dd_t[...])):
            placed = ones_where(here & (lane == hid - h * HH + n * HH))
            term = dot(part, placed)
            total = term if total is None else total + term
        pack[h] = total.astype(BF16)

    pl.semaphore_wait(
        barrier, jnp.where(own_half, 7, 8) + 8 + 4 + EXPERTS
    )

    def dispatch(h, k):
        to_x, to_z = dest_of(b, k)
        slot = (k % 2) * 4 + xl * 2 + core
        return remote(
            sbuf.at[h, rows_of(k, SEND)], rbuf.at[h, rows_of(slot, SEND)],
            dis_send.at[h * 4 + k], dis_recv.at[h * 8 + slot], dev(b, to_x, to_z, b % 2),
        )

    @pl.loop(0, 4)
    def _(n):
        dispatch(0, n).start()

    fill(1)

    @pl.loop(0, 4)
    def _(n):
        dispatch(1, n).start()

    def cut_to(d):
        return remote(
            pair_of((y + d) % NY), wall.at[0, y], wa_send.at[d - 1], wa_recv.at[y], along_y(d)
        )

    for d in range(1, NY):
        cut_to(d).start()

    to_partner = [
        remote(pack.at[1 - core], theirs, core_send.at[0], core_recv.at[0], partner),
        remote(tok_half(xl), tq.at[pl.ds(NT, NT)], core_send.at[1], core_recv.at[1], partner),
        remote(wg_hbm, wg.at[1], core_send.at[2], core_recv.at[2], partner),
        remote(wu_hbm, wu.at[1], core_send.at[3], core_recv.at[3], partner),
    ]
    for copy in to_partner:
        copy.start()
    tok_across = remote(
        tok_half(1 - xl), tq.at[pl.ds(2 * NT, NT)], ac_send.at[0], ac_recv.at[0], across
    )
    tok_across.start()

    place = iota((EXPERTS * BACK, NT), 0)
    hit0 = routes_t[0:1, :] == place // BACK
    hit1 = routes_t[1:2, :] == place // BACK
    rank_all = dot(ones_where(hit0 | hit1), before)
    share = jnp.where(hit0, weights_t[0:1, :], 0.0) + jnp.where(hit1, weights_t[1:2, :], 0.0)
    share = jnp.where(rank_all == ((place % BACK) % CAP).astype(F32), share, 0.0).T
    back_tile = (iota((NT, EXPERTS * BACK), 1) % BACK) // CAP
    for n in range(4):
        mine = jnp.where(back_tile == n, share, 0.0)
        mine_hi = mine.astype(BF16)
        shares[0, n * NT:(n + 1) * NT] = mine_hi
        shares[1, n * NT:(n + 1) * NT] = (mine - mine_hi.astype(F32)).astype(BF16)

    to_partner[0].wait_recv()
    mine = pack[core]
    first = jnp.where(core == 0, mine, theirs[...])
    second = jnp.where(core == 0, theirs[...], mine)
    dense_w[pl.ds(pl.multiple_of(z * CHIP_ROWS, 16), CHIP_ROWS), :] = jnp.concatenate(
        [first, second], axis=0
    )

    def block_rows(yy):
        return pl.ds(pl.multiple_of(yy * BLOCK, 16), BLOCK)

    def x_part(yy, h):
        return xbuf.at[block_rows(yy), pl.ds(pl.multiple_of(h * HALF, 128), HALF)]

    def wait_spread(yy, h):
        remote(
            x_part(yy, h), x_part(yy, h), bx_send.at[0], bc_recv.at[h * NY + yy], partner
        ).wait_recv()

    def spread_x(yy, h):
        return remote(
            x_part(yy, h), x_part(yy, h), bx_send.at[h * NY + yy], bc_recv.at[h * NY + yy],
            across_hi,
        )

    def spread_y(h, n):
        return remote(
            x_part(y, h), x_part(y, h), by_send.at[3 * h + n], bc_recv.at[h * NY + y],
            along_y((1, 3, 2)[n]),
        )

    def pass_on(h):
        yy = (y + 3 - 2 * h) % NY
        return remote(
            x_part(yy, h), x_part(yy, h), bp_send.at[h], bc_recv.at[h * NY + yy],
            along_y(1 + 2 * h),
        )

    def shard(zz, p):
        return dense_w.at[
            pl.ds(pl.multiple_of(zz * CHIP_ROWS, 16), CHIP_ROWS),
            pl.ds(p * PIECE, PIECE),
        ]

    def go_right(k, p):
        s = shard((z + NZ - k) % NZ, p)
        return remote(s, s, right_send.at[2 * k + p], right_recv.at[2 * k + p], up_z)

    def go_left(k, p):
        s = shard((z + k) % NZ, p)
        return remote(s, s, left_send.at[2 * k + p], left_recv.at[2 * k + p], down_z)

    def ring_step(k):
        for p in range(2):
            go_right(k - 1, p).wait_recv()
            go_right(k, p).start()
            go_left(k - 1, p).wait_recv()

            @pl.when(k < 7)
            def _():
                go_left(k, p).start()

    for p in range(2):
        go_right(0, p).start()
        go_left(0, p).start()

    @pl.when(active)
    def _():
        slot_row = iota((BLOCK, 8 * SEND), 0)
        offset = iota((BLOCK, 8 * SEND), 1) - (slot_row // CAP) * SEND - slot_row % CAP
        for n in range(TILES):
            squeeze[n * BLOCK:(n + 1) * BLOCK] = ones_where(offset == n * CAP)

        for h in range(2):

            @pl.loop(0, 8)
            def _(s):
                remote(
                    sbuf.at[h, rows_of(0, SEND)], rbuf.at[h, rows_of(s, SEND)],
                    dis_send.at[0], dis_recv.at[h * 8 + s], partner,
                ).wait_recv()

            rows = dot(squeeze[...], rbuf[h]).astype(BF16)
            for n in range(TILES):
                xbuf[block_rows(y), h * HALF + n * TILE:h * HALF + (n + 1) * TILE] = rows[
                    n * BLOCK:(n + 1) * BLOCK
                ]

            spread_x(y, h).start()
            for n in range(2 + h):
                spread_y(h, n).start()

    relay = remote(
        tq.at[pl.ds(2 * NT, NT)], tq.at[pl.ds(3 * NT, NT)], core_send.at[5], core_recv.at[5],
        partner,
    )

    @pl.when(jnp.logical_not(active))
    def _():
        ring_step(1)
        wait_spread(y, 0)
        for n in range(2):
            spread_y(0, n).start()

    for copy in local[1:4]:
        copy.wait()
    for copy in to_partner[2:4]:
        copy.wait_recv()

    wall_partner = remote(
        wall.at[0], wall.at[1], core_send.at[4], core_recv.at[4], partner
    )

    def hid_y(g, d):
        return remote(
            hcat.at[y, g], hcat.at[y, g], hy_send.at[3 * g + d - 1], hy_recv.at[g * NY + y],
            along_y(d),
        )

    def wait_hid(yy, g):
        remote(
            hcat.at[yy, g], hcat.at[yy, g], hy_send.at[0], hy_recv.at[g * NY + yy], partner
        ).wait_recv()

    def gate_up(h):
        cols = pl.ds(h * HALF, HALF)
        x = xbuf[:, cols]
        return [dot_nt(x, w[half, :, cols]) for half in range(2) for w in (wg, wu)]

    def experts_first():
        wait_spread((y + 1) % NY, 0)
        wait_spread((y + 2) % NY, 0)
        for n, part in enumerate(gate_up(0)):
            acc[n] = part

    def experts_second():
        @pl.when(jnp.logical_not(active))
        def _():
            for d in range(NY):
                wait_spread((y + d) % NY, 1)

        parts = [acc[n] + part for n, part in enumerate(gate_up(1))]
        hidden = jnp.concatenate(
            [
                (silu(parts[2 * half]) * parts[2 * half + 1]).astype(BF16)
                for half in range(2)
            ],
            axis=1,
        )
        for g in range(2):
            hcat[y, g] = hidden[g * 2 * BLOCK:(g + 1) * 2 * BLOCK]
            for d in range(1, NY):
                hid_y(g, d).start()

    wide_row = iota((8 * BACK, BLOCK), 0)
    wide_at = wide_row % BACK
    wide_tile = jnp.where(
        (wide_row // BACK) * CAP + wide_at % CAP == iota((8 * BACK, BLOCK), 1),
        wide_at // CAP, -1,
    )
    widen = [ones_where(wide_tile == n) for n in range(4)]

    def give(yy, s):
        s_x, s_z, s_c = source_of(2 * yy + core, s)
        return remote(
            tbuf.at[yy, rows_of(s, BACK)], ret.at[rows_of(chip, BACK)], ret_send.at[yy * 8 + s],
            ret_recv.at[chip], dev(b, s_x, s_z, s_c),
        )

    def cross_x(g):
        return remote(cross.at[g], crossed.at[g], cx_send.at[g], cx_recv.at[g], across_hi)

    def outputs(g):
        for d in range(1, NY):
            wait_hid((y + d) % NY, g)
        total = None
        for yy in range(NY):
            value = hcat[yy, g]
            for half in range(2):
                part = dot(value[:, half * HH:(half + 1) * HH], wall[half, yy])
                total = part if total is None else total + part
        low, high = total[:, 0:COLS], total[:, COLS:2 * COLS]
        keep[g] = jnp.where(side == 0, low, high)
        cross[g] = jnp.where(side == 0, high, low).astype(BF16)
        cross_x(g).start()

    def finish_outputs(g):
        cross_x(g).wait_recv()
        total = keep[g] + crossed[g].astype(F32)
        total = jnp.concatenate(
            [total.astype(BF16), jnp.zeros((2 * BLOCK, 4 * TILE - COLS), BF16)], axis=1
        )
        for i in range(2):
            wide = None
            for n in range(4):
                part = dot(
                    widen[n], total[i * BLOCK:(i + 1) * BLOCK, n * TILE:(n + 1) * TILE]
                )
                wide = part if wide is None else wide + part
            tbuf[2 * g + i] = wide.astype(BF16)

            @pl.loop(0, 8)
            def _(s):
                give(2 * g + i, s).start()

    @pl.when(active)
    def _():
        ring_step(1)

    ring_step(2)

    @pl.loop(3, 8)
    def _(k):
        @pl.when((k == 3) & active)
        def _():
            wait_spread((y + 3) % NY, 0)
            pass_on(0).start()
            wait_spread((y + 1) % NY, 1)
            spread_x((y + 1) % NY, 1).start()
            wait_spread((y + 3) % NY, 1)
            spread_x((y + 3) % NY, 1).start()

        ring_step(k)

        @pl.when((k == 3) & jnp.logical_not(active))
        def _():
            wait_spread((y + 3) % NY, 0)
            pass_on(0).start()

        @pl.when((k == 4) & active)
        def _():
            wait_spread((y + 2) % NY, 1)
            spread_x((y + 2) % NY, 1).start()

        @pl.when(k == jnp.where(active, 5, 6))
        def _():
            experts_first()
            experts_second()

        @pl.when(k == 6)
        def _():
            for d in range(1, NY):
                src = (y + d) % NY
                remote(
                    pair_of(0), wall.at[0, src], wa_send.at[0], wa_recv.at[src], partner
                ).wait_recv()
            wall_partner.start()
            tok_across.wait_recv()
            relay.start()

    for p in range(2):
        go_right(7, p).wait_recv()

    local[4].wait()
    to_partner[1].wait_recv()
    relay.wait_recv()
    both = dot(tq[...], dense_w[:, 0:384])
    gu[...] = both[0:2 * NT]
    gu_send[...] = both[2 * NT:4 * NT].astype(BF16)
    gu_across = remote(gu_send, gu_recv, ac_send.at[1], ac_recv.at[1], across)
    gu_across.start()

    wall_partner.wait_recv()
    outputs(0)

    gu_across.wait_recv()
    both = gu[...] + gu_recv[...].astype(F32)
    dense_hidden = silu(both) * pltpu.roll(both, 384 - HH, 1)
    dense_hidden = jnp.where(iota((2 * NT, 384), 1) < HH, dense_hidden, 0.0)
    hbuf[0:2 * NT] = pltpu.roll(dense_hidden, 2 * HH - 256, 1)[:, 0:256].astype(BF16)
    h_across = remote(
        hbuf.at[pl.ds(0, 2 * NT)], hbuf.at[pl.ds(2 * NT, 2 * NT)], ac_send.at[2], ac_recv.at[2],
        across,
    )
    h_across.start()
    outputs(1)

    def dense_down(t):
        for n in range(HALF // PIECE):
            cols = pl.ds(n * PIECE, PIECE)
            part = dot_nt(
                hbuf[2 * t * NT:2 * (t + 1) * NT], dense_w[n * PIECE:(n + 1) * PIECE, 256:512]
            )
            d_mine[t, :, cols] = part[0:NT]
            d_send[t, :, cols] = part[NT:2 * NT].astype(BF16)

    swaps = [
        remote(d_send.at[t], d_recv.at[t], core_send.at[6 + t], core_recv.at[6 + t], partner)
        for t in range(2)
    ]
    def finish(t, q):
        to = 4 * xl + q
        to_x = (xl + t) % 2
        return remote(
            dterm.at[t, q], fin.at[b], fin_send.at[t * 4 + q], fin_recv.at[b],
            dev(to, to_x, z, core),
        )

    def others(t, q):
        return jnp.logical_not(own_half & (t == 0) & (4 * xl + q == b))

    def dense_out(t):
        swaps[t].wait_recv()
        for n in range(2):
            cols = pl.ds(n * 2 * COLS, 2 * COLS)
            value = (d_mine[t, :, cols] + d_recv[t, :, cols].astype(F32)).astype(BF16)
            dterm[t, 2 * n] = value[:, 0:COLS]
            dterm[t, 2 * n + 1] = value[:, COLS:2 * COLS]
            for q in (2 * n, 2 * n + 1):
                @pl.when(others(t, q))
                def _():
                    finish(t, q).start()

    dense_down(0)
    swaps[0].start()
    finish_outputs(0)
    dense_out(0)
    h_across.wait_recv()
    dense_down(1)
    swaps[1].start()
    finish_outputs(1)
    dense_out(1)

    @pl.when(own_half)
    def _():
        fin[b] = dterm[0, b % 4]

    for copy in to_partner:
        copy.wait_send()
    for copy in (tok_across, relay, gu_across, h_across, *swaps):
        copy.wait_send()

    @pl.loop(0, 8)
    def _(n):
        dispatch(n // 4, n % 4).wait_send()

        for p in range(2):
            go_right(n, p).wait_send()

            @pl.when(n < 7)
            def _():
                go_left(n, p).wait_send()

    wall_partner.wait_send()

    for d in range(1, NY):
        cut_to(d).wait_send()

    for g in range(2):
        cross_x(g).wait_send()
        for d in range(1, NY):
            hid_y(g, d).wait_send()

    pass_on(0).wait_send()
    for n in range(2):
        spread_y(0, n).wait_send()

    @pl.when(active)
    def _():
        spread_x(y, 0).wait_send()
        for n in range(3):
            spread_y(1, n).wait_send()
        for d in range(NY):
            spread_x((y + d) % NY, 1).wait_send()

    @pl.loop(0, EXPERTS)
    def _(e):
        remote(
            tbuf.at[0, rows_of(0, BACK)], ret.at[rows_of(e, BACK)], ret_send.at[0],
            ret_recv.at[e], partner,
        ).wait_recv()

    rows = ret[...]
    total = dot(shares[0], rows) + dot(shares[1], rows)
    total = jnp.concatenate([total[n * NT:(n + 1) * NT] for n in range(4)], axis=1)[:, 0:COLS]

    @pl.loop(0, NDP)
    def _(k):
        @pl.when(jnp.logical_not(own_half & (k == b)))
        def _():
            remote(
                dterm.at[0, 0], fin.at[k], fin_send.at[0], fin_recv.at[k], partner
            ).wait_recv()

    for k in range(NDP):
        total = total + fin[k].astype(F32)
    out[...] = total.T.astype(BF16)

    @pl.loop(0, 8)
    def _(n):
        @pl.when(others(n // 4, n % 4))
        def _():
            finish(n // 4, n % 4).wait_send()

    @pl.loop(0, EXPERTS)
    def _(n):
        give(n // 8, n % 8).wait_send()


def per_device(
    tokens, routes, gate_weights, w_dense_gate, w_dense_up, w_dense_down,
    w_exp_gate, w_exp_up, w_exp_down,
):
    rows = w_dense_gate.shape[0]
    vmem = pl.BlockSpec(memory_space=pltpu.VMEM)
    hbm = pl.BlockSpec(memory_space=pl.ANY)
    dma = pltpu.SemaphoreType.DMA
    out_t = pl.pallas_call(
        kernel,
        out_shape=jax.ShapeDtypeStruct((COLS, NT), BF16),
        in_specs=[vmem] * 5 + [hbm] * 4,
        out_specs=vmem,
        scratch_shapes=[
            pltpu.VMEM((NT, D), BF16),
            pltpu.VMEM((4 * NT, HALF), BF16),
            pltpu.VMEM((2, 4 * SEND, TILE), BF16),
            pltpu.VMEM((2, 8 * SEND, TILE), BF16),
            pltpu.VMEM((TILES * BLOCK, 8 * SEND), BF16),
            pltpu.VMEM((2, 4 * NT, EXPERTS * BACK), BF16),
            pltpu.VMEM((NY * BLOCK, D), BF16),
            pltpu.VMEM((NY, 2, 2 * BLOCK, 2 * HH), BF16),
            pltpu.VMEM((2, 2 * BLOCK, COLS), F32),
            pltpu.VMEM((2, 2 * BLOCK, COLS), BF16),
            pltpu.VMEM((2, 2 * BLOCK, COLS), BF16),
            pltpu.VMEM((NY, 8 * BACK, TILE), BF16),
            pltpu.VMEM((EXPERTS * BACK, TILE), BF16),
            pltpu.VMEM((2, HH, D), BF16),
            pltpu.VMEM((2, HH, D), BF16),
            pltpu.VMEM((2, NY, HH, 2 * COLS), BF16),
            pltpu.VMEM((2, rows, CHUNK), BF16),
            pltpu.VMEM((rows, CHUNK), BF16),
            pltpu.VMEM((HALF, CHUNK), BF16),
            pltpu.VMEM((4, NY * BLOCK, HH), F32),
            pltpu.VMEM((2 * NT, 384), F32),
            pltpu.VMEM((2 * NT, 384), BF16),
            pltpu.VMEM((2 * NT, 384), BF16),
            pltpu.VMEM((4 * NT, 256), BF16),
            pltpu.VMEM((2, NT, HALF), F32),
            pltpu.VMEM((2, NT, HALF), BF16),
            pltpu.VMEM((2, NT, HALF), BF16),
            pltpu.VMEM((2, 4, NT, COLS), BF16),
            pltpu.VMEM((NDP, NT, COLS), BF16),
            dma((5,)), dma((8,)), dma((8,)), dma((3,)), dma((3,)), dma((8,)), dma((16,)),
            dma((8,)), dma((6,)), dma((2,)), dma((8,)),
            dma((16,)), dma((16,)), dma((14,)), dma((14,)),
            dma((3,)), dma((4,)), dma((2,)), dma((2,)), dma((6,)), dma((8,)),
            dma((32,)), dma((32,)),
            dma((8,)), dma((8,)),
        ],
        compiler_params=pltpu.CompilerParams(
            collective_id=0, has_side_effects=True, vmem_limit_bytes=56 * 1024 * 1024
        ),
    )(
        routes.T, gate_weights.T, w_dense_gate, w_dense_up, w_dense_down.T, tokens,
        w_exp_gate[0, 0].T, w_exp_up[0, 0].T, w_exp_down[0, 0],
    )
    return out_t.T


def solution(mesh):
    in_specs = (
        P("expert", None),
        P("expert", None),
        P("expert", None),
        P("expert", "dp"),
        P("expert", "dp"),
        P("dp", "expert"),
        P("dp", "expert", None, None),
        P("dp", "expert", None, None),
        P("dp", "expert", None, None),
    )
    return jax.shard_map(
        per_device, mesh=mesh, in_specs=in_specs, out_specs=P("expert", "dp"), check_vma=False
    )
```
